512 devices in a mesh: tile: 64 (over x, z, core), tm: 8 (over y).
Axes of the slice: x: 4, y: 8, z: 8, core: 2. Of those that a mesh axis runs over, the one named last changes fastest.
Arguments:
- model: bfloat16 [2, 16384, 1024], P(None, ('tile', 'tm')), may hold values from -6 to 6
- kern_rows: bfloat16 [24576, 32, 256], P(('tile', 'tm')), may hold values from -1 to 1
- kern_cols: bfloat16 [24576, 128, 256], P(('tile', 'tm')), may hold values from -0.5 to 0.5
- visibilities: bfloat16 [24576, 2, 256], P(('tile', 'tm')), may hold values from -6 to 6
- owner_tile: int32 [24576, 1], P(('tile', 'tm')), may hold values from 0 to 63; in each aligned block of 48 rows (0 to 47, 48 to 95, ...) at most 2 rows name the same one
- row_offset: int32 [24576], P(('tile', 'tm')), may hold values from 0 to 224
- col_offset: int32 [24576], P(('tile', 'tm')), may hold values from 0 to 896
Outputs:
- dirty_grid: float32 [2, 16384, 1024], P(None, ('tile', 'tm'))
- residual_vis: float32 [24576, 2, 256], P(('tile', 'tm'))
The draws below stay inside these ranges and needn't reach their ends.
Inputs may be any that keep to these rules, and one draw needn't show every extreme that they name: `owner_tile`: among the 48 blocks of one device no tile is named more than 2 times, and some device names a tile exactly 2 times.
All inputs are finite; a program needn't handle non-finite values.
Results may differ from the reference program's by a relative error of at most 0.0026.
Values may be sent and summed in bfloat16 or wider, within the bound.
A program may use at most 128 MiB of HBM per device.

```python
import math
import jax
import jax.numpy as jnp
import numpy as np
from jax import lax

SU = 32
SV = 128
VB = 256
TU = 256
GV = 1024
NB = 48
CAP = 2
GU = 16384
BLOCKS = 24576
N_TILE = 64


def plant(array, own_key, smallest, high):
    longest = array.shape.index(max(array.shape))
    spots = []
    for shift in (0, 1):
        where = [jax.random.randint(jax.random.fold_in(own_key, axis), (), 0, length) for axis, length in enumerate(array.shape)]
        where[longest] = (where[longest] + shift) % array.shape[longest]
        spots.append(tuple(where))
    return array.at[spots[0]].set(smallest).at[spots[1]].set(high)


def steps_of(stream_key, shape, split, low, largest):
    def one(position, parts):
        steps = jax.random.uniform(jax.random.fold_in(jax.random.fold_in(stream_key, 6), position), (parts,), jnp.float32, low / len(split), largest / len(split))
        return jnp.repeat(jnp.exp(steps), shape[position] // parts).reshape((-1,) + (1,) * (len(shape) - position - 1))

    gain = one(*split[0])
    for cut in split[1:]:
        gain = gain * one(*cut)
    return gain


def shared_out(stream_key, own, number, rows, number_of, top, reach, slope):
    order = jax.random.permutation(stream_key, number_of)
    crowded, ordinary = portions_of(number_of, rows * top, reach, slope, True), portions_of(number_of, rows * top, reach, slope, False)
    places = jnp.arange(number_of)

    def named(sizes, rotation):
        used = int((sizes > 0).sum())
        fixed = max(1, used // 4)
        passed = fixed + (places - fixed + rotation * (used - fixed)) % max(1, number_of - fixed)
        return jnp.zeros((number_of,), jnp.int32).at[order[jnp.where(places < fixed, places, passed)]].set(jnp.asarray(sizes, jnp.int32))

    sizes = jnp.where(number % 4 == 0, named(crowded, number // 4), named(ordinary, number - number // 4 - 1))
    mixed = jax.random.permutation(jax.random.fold_in(own, 3), number_of)
    giver, sink = mixed[0:number_of // 2 * 2:2], mixed[1:number_of // 2 * 2:2]
    slack = jnp.minimum(sizes[giver] - 1, reach - sizes[sink]) // 2
    slack = jnp.where((giver == order[0]) | (sink == order[0]) | (sizes[sink] == 0), 0, jnp.maximum(slack, 0))
    passed = jax.random.randint(jax.random.fold_in(own, 4), (number_of // 2,), 0, 1 << 20) % (slack + 1)
    sizes = sizes.at[giver].add(-passed).at[sink].add(passed)
    members = jnp.searchsorted(jnp.cumsum(sizes), jnp.arange(rows * top), side="right").astype(jnp.int32)
    grid = members.reshape(top, rows).T
    grid = grid[jax.random.permutation(jax.random.fold_in(own, 1), rows)]
    rotation = jax.random.randint(jax.random.fold_in(own, 2), (rows, 1), 0, top)
    return jnp.take_along_axis(grid, (jnp.arange(top)[None, :] + rotation) % top, axis=1)


def portions_of(number_of, total, limit, lean, full):
    weights = [(1 << 20) // math.isqrt(standing ** lean) + 1 for standing in range(1, number_of + 1)]
    largest = limit if full else min(limit, max(-(-total // number_of), total * weights[0] // sum(weights)))
    least = 1 if total - largest >= number_of - 1 else 0
    given, spare = [largest] + [least] * (number_of - 1), total - largest - least * (number_of - 1)
    while spare > 0:
        candidates = [i for i in range(1, number_of) if given[i] < largest] or [i for i in range(1, number_of) if given[i] < limit]
        mass, remaining = sum([weights[i] for i in candidates]), spare
        for i in candidates:
            more = min(limit - given[i], max(1, remaining * weights[i] // mass), spare)
            given[i] = given[i] + more
            spare = spare - more
    return np.array(given)


def centred(rng, dims, width, limit, cuts=(), kind=jnp.bfloat16):
    result = jax.random.normal(rng, dims, jnp.float32) * width
    if len(cuts) > 0:
        result = steps_of(rng, dims, cuts, -0.22, 0.18) * result
    return jnp.clip(result, min=-limit, max=limit).astype(kind)


def setup_inputs(seed: int = 0) -> dict:
    streams_of = jax.random.split(jax.random.key(seed), 8)
    model = centred(streams_of[0], (2, GU, GV), 1.0, 6.0, ((1, 512),))
    kern_rows = centred(streams_of[1], (BLOCKS, SU, VB), SU ** -0.5, 1.0, ((0, 512),))
    kern_cols = centred(streams_of[2], (BLOCKS, SV, VB), SV ** -0.5, 0.5, ((0, 512),))
    visibilities = centred(streams_of[3], (BLOCKS, 2, VB), 1.0, 6.0, ((0, 512),))
    owner_tile_keys = jax.random.split(jax.random.fold_in(streams_of[4], 1), BLOCKS // NB)
    owner_tile_turns = jax.random.permutation(jax.random.fold_in(streams_of[4], 3), BLOCKS // NB)
    owner_tile = jax.vmap(lambda own, number: shared_out(jax.random.fold_in(streams_of[4], 2), own, number, NB, N_TILE, 1, CAP, 2))(owner_tile_keys, owner_tile_turns).reshape((BLOCKS, 1))
    row_offset = plant(jax.random.randint(streams_of[5], (BLOCKS,), 0, TU - SU + 1), jax.random.fold_in(streams_of[5], 1), 0, TU - SU).astype(jnp.int32)
    col_offset = plant(jax.random.randint(streams_of[6], (BLOCKS,), 0, GV - SV + 1), jax.random.fold_in(streams_of[6], 1), 0, GV - SV).astype(jnp.int32)
    return dict(model=model, kern_rows=kern_rows, kern_cols=kern_cols, visibilities=visibilities, owner_tile=owner_tile, row_offset=row_offset, col_offset=col_offset)


def degrid_regrid(patches, kern_rows, kern_cols, visibilities):
    sampled = jnp.einsum('scuv,svj->scuj', patches.astype(jnp.float32), kern_cols.astype(jnp.float32))
    row_weights = kern_rows.astype(jnp.float32)[:, None]
    predicted = jnp.sum(row_weights * sampled, axis=2)
    residual = visibilities.astype(jnp.float32) - predicted
    weighted = (row_weights * residual[:, :, None, :]).astype(jnp.bfloat16)
    subgrid = jnp.einsum('scuj,svj->scuv', weighted.astype(jnp.float32), kern_cols.astype(jnp.float32))
    return residual, subgrid


def extract(grid_part, row_at, col_at):
    anchor = jnp.zeros((), jnp.int32)
    def single(row_one, col_one):
        return lax.dynamic_slice(grid_part, (anchor, row_one, col_one), (2, SU, SV))
    return jax.vmap(single)(row_at, col_at)


def add_patches(total, subgrids, row_at, col_at):
    row_index = row_at[:, None, None] + jnp.arange(SU).astype(jnp.int32)[None, :, None]
    col_index = col_at[:, None, None] + jnp.arange(SV).astype(jnp.int32)[None, None, :]
    return total.at[:, row_index, col_index].add(jnp.moveaxis(subgrids, 1, 0))


def reference(model, kern_rows, kern_cols, visibilities, owner_tile, row_offset, col_offset):
    owners = owner_tile[:, 0].astype(jnp.int32)
    row_start = (owners * TU + row_offset).astype(jnp.int32)
    col_start = col_offset.astype(jnp.int32)
    batch_size = math.gcd(BLOCKS, 256)
    batches = BLOCKS // batch_size

    def shaped(values):
        return values.reshape((batches, batch_size) + values.shape[1:])

    def add_batch(grid_sum, batch_items):
        rows_k, cols_k, vis_k, row_at, col_at = batch_items
        patches = extract(model, row_at, col_at)
        residual, subgrid = degrid_regrid(patches, rows_k, cols_k, vis_k)
        return add_patches(grid_sum, subgrid, row_at, col_at), residual

    start_grid = jnp.zeros((2, GU, GV), jnp.float32)
    dirty_grid, residual = lax.scan(add_batch, start_grid, (shaped(kern_rows), shaped(kern_cols), shaped(visibilities), shaped(row_start), shaped(col_start)))
    return dirty_grid, residual.reshape((BLOCKS, 2, VB))
```

```python
import functools

import jax
import jax.numpy as jnp
from jax import lax
from jax.experimental import pallas as pl
from jax.experimental.pallas import tpu as pltpu
from jax.sharding import PartitionSpec as P

VMEM_LIMIT = 48 * 1024 * 1024


def corner(row, col, shape, sub_rows, sub_cols):
    top = jnp.minimum(row // 8, (shape[0] - sub_rows) // 8 - 1) * 8
    base = jnp.minimum(col // sub_cols, shape[1] // sub_cols - 2) * sub_cols
    return pl.multiple_of(top, 8), row - top, pl.multiple_of(base, sub_cols), col - base


def extract_kernel(req_ref, panel_ref, *rest, slots, shards):
    outs, wide = rest[:slots], rest[slots]
    sub_rows, sub_cols = outs[0].shape[2], outs[0].shape[3]
    shard_rows = panel_ref.shape[2]
    tiles = outs[0].shape[0]
    for m in range(shards):
        wide[:, m * shard_rows : (m + 1) * shard_rows, :] = panel_ref[m].astype(jnp.float32)
    for s in range(slots):

        @pl.loop(0, tiles, unroll=2)
        def _(o):
            row = jnp.maximum(req_ref[(o * slots + s) * 2], 0)
            col = jnp.maximum(req_ref[(o * slots + s) * 2 + 1], 0)
            top, down, base, right = corner(row, col, wide.shape[1:], sub_rows, sub_cols)
            for c in range(2):
                window = wide[c, pl.ds(top, sub_rows + 8), pl.ds(base, 2 * sub_cols)]
                window = pltpu.roll(window, lax.rem(sub_rows + 8 - down, sub_rows + 8), 0)[:sub_rows]
                window = pltpu.roll(window, lax.rem(2 * sub_cols - right, 2 * sub_cols), 1)
                outs[s][o, c] = window[:, :sub_cols].astype(jnp.bfloat16)


def block_kernel(order_ref, count_ref, patch_ref, rows_ref, cols_ref, vis_ref, *rest, step):
    sub_ref, res_ref = rest[-2:]
    sub_rows, sub_cols = patch_ref.shape[2], patch_ref.shape[3]
    vis_n = rows_ref.shape[2]
    if len(rest) == 3:
        res_ref[...] = rest[0][...]

    @pl.loop(0, count_ref[0])
    def _(i):
        for k in range(step):
            b = order_ref[2 * (i * step + k)]
            o = order_ref[2 * (i * step + k) + 1]
            patch = patch_ref[o].reshape(2 * sub_rows, sub_cols)
            cols = cols_ref[b]
            sampled = jnp.dot(patch, cols, preferred_element_type=jnp.float32)
            weights = rows_ref[b].astype(jnp.float32)
            sampled = sampled.reshape(2, sub_rows, vis_n)
            predicted = jnp.sum(weights[None] * sampled, axis=1)
            residual = vis_ref[b].astype(jnp.float32) - predicted
            res_ref[b] = residual
            weighted = (weights[None] * residual[:, None, :]).astype(jnp.bfloat16)
            weighted = weighted.reshape(2 * sub_rows, vis_n)
            sub = lax.dot_general(
                weighted, cols, (((1,), (1,)), ((), ())), preferred_element_type=jnp.float32
            )
            sub_ref[o] = sub.astype(jnp.bfloat16).reshape(2, sub_rows, sub_cols)


def add_kernel(req_ref, *rest, slots):
    subs, acc = rest[:slots], rest[slots]
    sub_rows, sub_cols = subs[0].shape[2], subs[0].shape[3]
    tiles = subs[0].shape[0]
    acc[...] = jnp.zeros_like(acc)
    for s in range(slots):

        @pl.loop(0, tiles)
        def _(o):
            row = req_ref[(o * slots + s) * 2]
            col = req_ref[(o * slots + s) * 2 + 1]

            @pl.when(row >= 0)
            def _():
                top, down, base, right = corner(row, col, acc.shape[1:], sub_rows, sub_cols)
                for c in range(2):
                    sub = subs[s][o, c].astype(jnp.float32)
                    window = jnp.concatenate([sub, jnp.zeros_like(sub)], axis=1)
                    window = pltpu.roll(window, right, 1)
                    window = jnp.concatenate([window, jnp.zeros((8, 2 * sub_cols), jnp.float32)], axis=0)
                    window = pltpu.roll(window, down, 0)
                    at = (c, pl.ds(top, sub_rows + 8), pl.ds(base, 2 * sub_cols))
                    acc[at] = acc[at] + window


def smem():
    return pl.BlockSpec(memory_space=pltpu.SMEM)


def vmem():
    return pl.BlockSpec(memory_space=pltpu.VMEM)


def shards(model, kern_rows, kern_cols, visibilities, owner_tile, row_offset, col_offset):
    tiles = lax.axis_size("tile")
    blocks = owner_tile.shape[0]
    slots = (blocks + tiles - 1) // tiles + 1
    sub_rows = kern_rows.shape[1]
    sub_cols = kern_cols.shape[1]
    grid_cols = model.shape[2]
    params = pltpu.CompilerParams(vmem_limit_bytes=VMEM_LIMIT)
    step = 4

    owners = owner_tile[:, 0]
    ids = jnp.arange(blocks, dtype=jnp.int32)
    earlier = (owners[:, None] == owners[None, :]) & (ids[None, :] < ids[:, None])
    slot_of = jnp.sum(earlier.astype(jnp.int32), axis=1)
    hot = (
        (owners[None, None, :] == jnp.arange(tiles, dtype=jnp.int32)[:, None, None])
        & (slot_of[None, None, :] == jnp.arange(slots, dtype=jnp.int32)[None, :, None])
    ).astype(jnp.int32)
    request = (
        jnp.stack(
            [
                jnp.sum(hot * (row_offset + 1)[None, None, :], axis=2),
                jnp.sum(hot * (col_offset + 1)[None, None, :], axis=2),
            ],
            axis=-1,
        )
        - 1
    )
    got = lax.all_to_all(request, "tile", split_axis=0, concat_axis=0, tiled=True).reshape(-1)
    panel = lax.all_gather(model, "tm", axis=0)
    group = panel.shape[0]

    patches = pl.pallas_call(
        functools.partial(extract_kernel, slots=slots, shards=group),
        out_shape=[jax.ShapeDtypeStruct((tiles, 2, sub_rows, sub_cols), jnp.bfloat16)] * slots,
        in_specs=[smem(), vmem()],
        out_specs=[vmem()] * slots,
        scratch_shapes=[pltpu.VMEM((2, group * model.shape[1], grid_cols), jnp.float32)],
        compiler_params=params,
        name="extract",
    )(got, panel)

    residual = None
    returned = []
    for s in range(slots):
        arrived = lax.all_to_all(patches[s], "tile", split_axis=0, concat_axis=0, tiled=True)
        mine = slot_of == s
        place = jnp.cumsum(mine.astype(jnp.int32)) - 1
        count = jnp.sum(mine.astype(jnp.int32))
        spots = jnp.arange(-(-blocks // step) * step, dtype=jnp.int32)
        wanted = jnp.minimum(spots, jnp.maximum(count - 1, 0))
        pick = (mine[None, :] & (place[None, :] == wanted[:, None])).astype(jnp.int32)
        order = jnp.stack([jnp.sum(pick * ids[None, :], axis=1), jnp.sum(pick * owners[None, :], axis=1)], axis=-1)
        turns = (count + step - 1) // step
        args = [order.reshape(-1), turns.reshape(1), arrived, kern_rows, kern_cols, visibilities]
        specs = [smem(), smem()] + [vmem()] * 4
        aliases = {}
        if residual is not None:
            args.append(residual)
            specs.append(vmem())
            aliases = {len(args) - 1: 1}
        sub, residual = pl.pallas_call(
            functools.partial(block_kernel, step=step),
            out_shape=[
                jax.ShapeDtypeStruct((tiles, 2, sub_rows, sub_cols), jnp.bfloat16),
                jax.ShapeDtypeStruct((blocks, 2, kern_rows.shape[2]), jnp.float32),
            ],
            in_specs=specs,
            out_specs=[vmem(), vmem()],
            input_output_aliases=aliases,
            compiler_params=params,
            name="blocks",
        )(*args)
        returned.append(lax.all_to_all(sub, "tile", split_axis=0, concat_axis=0, tiled=True))

    dirty = pl.pallas_call(
        functools.partial(add_kernel, slots=slots),
        out_shape=jax.ShapeDtypeStruct((2, group * model.shape[1], grid_cols), jnp.float32),
        in_specs=[smem()] + [vmem()] * slots,
        out_specs=vmem(),
        compiler_params=params,
        name="add",
    )(got, *returned)
    dirty_part = lax.psum_scatter(dirty, "tm", scatter_dimension=1, tiled=True)
    return (dirty_part, residual)


def solution(mesh):
    placed = (
        P(None, ("tile", "tm"), None),
        P(("tile", "tm"), None, None),
        P(("tile", "tm"), None, None),
        P(("tile", "tm"), None, None),
        P(("tile", "tm"), None),
        P(("tile", "tm")),
        P(("tile", "tm")),
    )
    return jax.shard_map(
        shards,
        mesh=mesh,
        in_specs=placed,
        out_specs=(P(None, ("tile", "tm"), None), P(("tile", "tm"), None, None)),
        check_vma=False,
    )
```

```python
import functools

import jax
import jax.numpy as jnp
from jax import lax
from jax.experimental import pallas as pl
from jax.experimental.pallas import tpu as pltpu
from jax.sharding import PartitionSpec as P

VMEM_LIMIT = 48 * 1024 * 1024
MESH = pl.DeviceIdType.MESH


def corner(row, col, shape, sub_rows, sub_cols):
    top = jnp.minimum(row // 8, (shape[0] - sub_rows) // 8 - 1) * 8
    base = jnp.minimum(col // sub_cols, shape[1] // sub_cols - 2) * sub_cols
    return pl.multiple_of(top, 8), row - top, pl.multiple_of(base, sub_cols), col - base


def major_kernel(
    tiles, group, slots,
    inv_ref, pos_ref, req_ref, model_ref, rows_hbm, cols_hbm, vis_hbm,
    back_ref, res_ref, asked,
    panel, cells, asked_s, patch_out, patch_in, sub_out, rows_ref, cols_ref, vis_ref, res_slots,
    kern_sem, smem_sem, ask_send, ask_recv, ring_send, ring_recv, patch_send, patch_recv, back_send, back_recv,
):
    me = lax.axis_index("tile")
    tm = lax.axis_index("tm")
    sub_rows, sub_cols = patch_in.shape[3], patch_in.shape[4]
    shard_rows = model_ref.shape[1]
    vis_n = rows_ref.shape[2]
    right, left = lax.rem(tm + 1, group), lax.rem(tm + group - 1, group)
    width = 3 if (tiles - 1) % 3 == 0 else 1

    loads = [
        pltpu.make_async_copy(src, dst, kern_sem.at[i])
        for i, (src, dst) in enumerate(((rows_hbm, rows_ref), (cols_hbm, cols_ref), (vis_hbm, vis_ref)))
    ]
    for load in loads:
        load.start()

    barrier = pltpu.get_barrier_semaphore()

    @pl.loop(1, tiles)
    def _(k):
        pl.semaphore_signal(barrier, inc=1, device_id=(lax.rem(me + k, tiles), tm), device_id_type=MESH)

    near = [right, left] if group > 2 else [right]
    for other in near:
        pl.semaphore_signal(barrier, inc=1, device_id=(me, other), device_id_type=MESH)
    pl.semaphore_wait(barrier, tiles - 1 + len(near))

    def to_tile(src, dst, send, recv, peer, mine):
        return pltpu.make_async_remote_copy(
            src_ref=src.at[peer], dst_ref=dst.at[mine], send_sem=send.at[peer], recv_sem=recv.at[mine],
            device_id=(peer, tm), device_id_type=MESH,
        )

    def ring(way, step, c):
        shard = lax.rem(tm - step + group, group) if way == 0 else lax.rem(tm + step, group)
        src = model_ref.at[c] if step == 0 else panel.at[shard, c]
        return pltpu.make_async_remote_copy(
            src_ref=src, dst_ref=panel.at[shard, c],
            send_sem=ring_send.at[way, step, c], recv_sem=ring_recv.at[way, step, c],
            device_id=(me, right if way == 0 else left), device_id_type=MESH,
        )

    hops = (group // 2, (group - 1) // 2)

    def arrived(way, step, c):
        shard = lax.rem(tm - step - 1 + group, group) if way == 0 else lax.rem(tm + step + 1, group)
        return pltpu.make_async_remote_copy(
            src_ref=panel.at[shard, c], dst_ref=panel.at[shard, c],
            send_sem=ring_send.at[way, step, c], recv_sem=ring_recv.at[way, step, c],
            device_id=(me, right if way == 0 else left), device_id_type=MESH,
        ), shard

    for c in range(2):
        for way in range(2):
            if hops[way] > 0:
                ring(way, 0, c).start()

    @pl.loop(1, tiles)
    def _(k):
        to_tile(req_ref, asked, ask_send, ask_recv, lax.rem(me + k, tiles), me).start()

    asked[me] = req_ref[me]

    def spread(c, shard, values):
        for h in range(shard_rows // 16):
            for t in range(values.shape[1] // sub_cols):
                cells[c, shard * (shard_rows // 16) + h, t] = values[
                    h * 16 : (h + 1) * 16, t * sub_cols : (t + 1) * sub_cols
                ]

    for c in range(2):
        spread(c, tm, model_ref[c])
    for step in range(hops[0]):
        for c in range(2):
            for way in range(2):
                if step < hops[way]:
                    copy, shard = arrived(way, step, c)
                    copy.wait_recv()
                    if step + 1 < hops[way]:
                        ring(way, step + 1, c).start()
                    spread(c, shard, panel[shard, c])

    @pl.loop(1, tiles)
    def _(k):
        peer = lax.rem(me + k, tiles)
        to_tile(asked, asked, ask_send, ask_recv, peer, peer).wait_recv()

    to_smem = pltpu.make_async_copy(asked, asked_s, smem_sem)
    to_smem.start()
    to_smem.wait()

    tall, broad = sub_rows + 16, 2 * sub_cols
    row_gap = lax.broadcasted_iota(jnp.int32, (sub_rows, tall), 1) - lax.broadcasted_iota(
        jnp.int32, (sub_rows, tall), 0
    )
    col_gap = lax.broadcasted_iota(jnp.int32, (broad, sub_cols), 0) - lax.broadcasted_iota(
        jnp.int32, (broad, sub_cols), 1
    )

    def cut(peer, target):
        for s in range(slots):
            row = jnp.maximum(asked_s[peer, 0, 2 * s], 0)
            col = jnp.maximum(asked_s[peer, 0, 2 * s + 1], 0)
            top = jnp.minimum(lax.div(row, 16), cells.shape[1] - tall // 16)
            base = jnp.minimum(lax.div(col, sub_cols), cells.shape[2] - 2)
            window = jnp.concatenate(
                [
                    jnp.concatenate([cells[c, top + i, base + j] for c in range(2) for j in range(2)], axis=1)
                    for i in range(tall // 16)
                ],
                axis=0,
            )
            pick_rows = (row_gap == row - 16 * top).astype(jnp.float32).astype(jnp.bfloat16)
            pick_cols = (col_gap == col - sub_cols * base).astype(jnp.float32).astype(jnp.bfloat16)
            window = jnp.dot(pick_rows, window, preferred_element_type=jnp.float32).astype(jnp.bfloat16)
            window = jnp.concatenate([window[:, :broad], window[:, broad:]], axis=0)
            window = jnp.dot(window, pick_cols, preferred_element_type=jnp.float32).astype(jnp.bfloat16)
            target[peer, s] = window.reshape(2, sub_rows, sub_cols)

    @pl.loop(0, (tiles - 1) // width)
    def _(i):
        peers = [lax.rem(me + 1 + i * width + w, tiles) for w in range(width)]
        for peer in peers:
            cut(peer, patch_out)
        for peer in peers:
            to_tile(patch_out, patch_in, patch_send, patch_recv, peer, me).start()

    cut(me, patch_in)
    for load in loads:
        load.wait()

    def work(peer, target):
        for s in range(slots):
            b = inv_ref[peer * slots + s]
            patch = patch_in[peer, s].reshape(2 * sub_rows, sub_cols)
            cols = cols_ref[b]
            sampled = jnp.dot(patch, cols, preferred_element_type=jnp.float32)
            weights = rows_ref[b].astype(jnp.float32)
            sampled = sampled.reshape(2, sub_rows, vis_n)
            predicted = jnp.sum(weights[None] * sampled, axis=1)
            residual = vis_ref[b].astype(jnp.float32) - predicted
            res_slots[peer * slots + s] = residual
            weighted = (weights[None] * residual[:, None, :]).astype(jnp.bfloat16)
            weighted = weighted.reshape(2 * sub_rows, vis_n)
            sub = lax.dot_general(
                weighted, cols, (((1,), (1,)), ((), ())), preferred_element_type=jnp.float32
            )
            target[peer, s] = sub.astype(jnp.bfloat16).reshape(2, sub_rows, sub_cols)

    work(me, back_ref)

    @pl.loop(0, (tiles - 1) // width)
    def _(i):
        peers = [lax.rem(me + tiles - 1 - i * width - w, tiles) for w in range(width)]
        for peer in peers:
            to_tile(patch_out, patch_in, patch_send, patch_recv, peer, peer).wait_recv()
        for peer in peers:
            work(peer, sub_out)
        for peer in peers:
            to_tile(sub_out, back_ref, back_send, back_recv, peer, me).start()

    @pl.loop(0, res_ref.shape[0], unroll=4)
    def _(b):
        res_ref[b] = res_slots[pos_ref[b]]

    for c in range(2):
        for way in range(2):
            for step in range(hops[way]):
                ring(way, step, c).wait_send()

    @pl.loop(1, tiles)
    def _(k):
        peer = lax.rem(me + k, tiles)
        to_tile(req_ref, asked, ask_send, ask_recv, peer, me).wait_send()
        to_tile(patch_out, patch_in, patch_send, patch_recv, peer, me).wait_send()
        to_tile(sub_out, back_ref, back_send, back_recv, peer, me).wait_send()
        to_tile(sub_out, back_ref, back_send, back_recv, peer, peer).wait_recv()


def add_kernel(req_ref, subs, acc, *, slots):
    tiles, sub_rows, sub_cols = subs.shape[0], subs.shape[3], subs.shape[4]
    acc[...] = jnp.zeros_like(acc)

    @pl.loop(0, tiles * slots)
    def _(i):
        row = req_ref[2 * i]
        col = req_ref[2 * i + 1]

        @pl.when(row >= 0)
        def _():
            top, down, base, right = corner(row, col, acc.shape[1:], sub_rows, sub_cols)
            for c in range(2):
                sub = subs[i // slots, lax.rem(i, slots), c].astype(jnp.float32)
                window = jnp.concatenate([sub, jnp.zeros_like(sub)], axis=1)
                window = pltpu.roll(window, right, 1)
                window = jnp.concatenate([window, jnp.zeros((8, 2 * sub_cols), jnp.float32)], axis=0)
                window = pltpu.roll(window, down, 0)
                at = (c, pl.ds(top, sub_rows + 8), pl.ds(base, 2 * sub_cols))
                acc[at] = acc[at] + window


def smem():
    return pl.BlockSpec(memory_space=pltpu.SMEM)


def vmem():
    return pl.BlockSpec(memory_space=pltpu.VMEM)


def anywhere():
    return pl.BlockSpec(memory_space=pl.ANY)


def shards(model, kern_rows, kern_cols, visibilities, owner_tile, row_offset, col_offset):
    tiles = lax.axis_size("tile")
    group = lax.axis_size("tm")
    blocks = owner_tile.shape[0]
    slots = (blocks + tiles - 1) // tiles + 1
    sub_rows = kern_rows.shape[1]
    sub_cols = kern_cols.shape[1]
    vis_n = kern_rows.shape[2]
    shard_rows, grid_cols = model.shape[1:]
    tile_rows = group * shard_rows

    owners = owner_tile[:, 0]
    ids = jnp.arange(blocks, dtype=jnp.int32)
    earlier = (owners[:, None] == owners[None, :]) & (ids[None, :] < ids[:, None])
    place = owners * slots + jnp.sum(earlier.astype(jnp.int32), axis=1)
    hot = (place[None, :] == jnp.arange(tiles * slots, dtype=jnp.int32)[:, None]).astype(jnp.int32)
    inverse = jnp.sum(hot * ids[None, :], axis=1)
    wanted = jnp.stack([row_offset, col_offset], axis=0)
    request = (jnp.sum(hot[:, None, :] * (wanted + 1)[None], axis=2) - 1).reshape(tiles, 1, slots * 2)
    request = jnp.pad(request, ((0, 0), (0, 0), (0, 128 - slots * 2)))

    pair = (tiles, slots, 2, sub_rows, sub_cols)
    hops = max(group // 2, 1)
    dma = pltpu.SemaphoreType.DMA
    returned, residual, asked = pl.pallas_call(
        functools.partial(major_kernel, tiles, group, slots),
        out_shape=[
            jax.ShapeDtypeStruct(pair, jnp.bfloat16),
            jax.ShapeDtypeStruct((blocks, 2, vis_n), jnp.float32),
            jax.ShapeDtypeStruct((tiles, 1, 128), jnp.int32),
        ],
        in_specs=[smem(), smem(), vmem(), vmem(), anywhere(), anywhere(), anywhere()],
        out_specs=[vmem(), vmem(), vmem()],
        scratch_shapes=[
            pltpu.VMEM((group, 2, shard_rows, grid_cols), jnp.bfloat16),
            pltpu.VMEM((2, tile_rows // 16, grid_cols // sub_cols, 16, sub_cols), jnp.bfloat16),
            pltpu.SMEM((tiles, 1, 128), jnp.int32),
            pltpu.VMEM(pair, jnp.bfloat16),
            pltpu.VMEM(pair, jnp.bfloat16),
            pltpu.VMEM(pair, jnp.bfloat16),
            pltpu.VMEM(kern_rows.shape, jnp.bfloat16),
            pltpu.VMEM(kern_cols.shape, jnp.bfloat16),
            pltpu.VMEM(visibilities.shape, jnp.bfloat16),
            pltpu.VMEM((tiles * slots, 2, vis_n), jnp.float32),
            dma((3,)),
            dma,
            dma((tiles,)),
            dma((tiles,)),
            dma((2, hops, 2)),
            dma((2, hops, 2)),
            dma((tiles,)),
            dma((tiles,)),
            dma((tiles,)),
            dma((tiles,)),
        ],
        compiler_params=pltpu.CompilerParams(
            collective_id=0, has_side_effects=True, vmem_limit_bytes=VMEM_LIMIT
        ),
        name="major",
    )(inverse, place, request, model, kern_rows, kern_cols, visibilities)

    dirty = pl.pallas_call(
        functools.partial(add_kernel, slots=slots),
        out_shape=jax.ShapeDtypeStruct((2, tile_rows, grid_cols), jnp.float32),
        in_specs=[smem(), vmem()],
        out_specs=vmem(),
        compiler_params=pltpu.CompilerParams(vmem_limit_bytes=VMEM_LIMIT),
        name="add",
    )(asked[:, 0, : slots * 2].reshape(-1), returned)
    dirty_part = lax.psum_scatter(dirty, "tm", scatter_dimension=1, tiled=True)
    return (dirty_part, residual)


def solution(mesh):
    placed = (
        P(None, ("tile", "tm"), None),
        P(("tile", "tm"), None, None),
        P(("tile", "tm"), None, None),
        P(("tile", "tm"), None, None),
        P(("tile", "tm"), None),
        P(("tile", "tm")),
        P(("tile", "tm")),
    )
    return jax.shard_map(
        shards,
        mesh=mesh,
        in_specs=placed,
        out_specs=(P(None, ("tile", "tm"), None), P(("tile", "tm"), None, None)),
        check_vma=False,
    )
```

```python
import functools

import jax
import jax.numpy as jnp
from jax import lax
from jax.experimental import pallas as pl
from jax.experimental.pallas import tpu as pltpu
from jax.sharding import PartitionSpec as P

VMEM_LIMIT = 48 * 1024 * 1024
MESH = pl.DeviceIdType.MESH


def major_kernel(
    tiles, group, slots,
    inv_ref, pos_ref, req_ref, model_ref, rows_hbm, cols_hbm, vis_hbm,
    out_ref, res_ref,
    asked, panel, cells, asked_s, patch_out, patch_in, sub_out, back_ref, rows_ref, cols_ref, vis_ref, res_slots,
    spread_ref, acc, sums,
    kern_sem, smem_sem, ask_send, ask_recv, ring_send, ring_recv, patch_send, patch_recv, back_send, back_recv,
    sum_send, sum_recv,
):
    me = lax.axis_index("tile")
    tm = lax.axis_index("tm")
    sub_rows, sub_cols = patch_in.shape[3], patch_in.shape[4]
    shard_rows = model_ref.shape[1]
    vis_n = rows_ref.shape[2]
    right, left = lax.rem(tm + 1, group), lax.rem(tm + group - 1, group)
    width = 3 if (tiles - 1) % 3 == 0 else 1

    loads = [
        pltpu.make_async_copy(src, dst, kern_sem.at[i])
        for i, (src, dst) in enumerate(((rows_hbm, rows_ref), (cols_hbm, cols_ref), (vis_hbm, vis_ref)))
    ]
    for load in loads:
        load.start()

    barrier = pltpu.get_barrier_semaphore()

    @pl.loop(1, tiles)
    def _(k):
        pl.semaphore_signal(barrier, inc=1, device_id=(lax.rem(me + k, tiles), tm), device_id_type=MESH)

    near = [right, left] if group > 2 else [right]
    for other in near:
        pl.semaphore_signal(barrier, inc=1, device_id=(me, other), device_id_type=MESH)
    pl.semaphore_wait(barrier, tiles - 1 + len(near))

    def to_tile(src, dst, send, recv, peer, mine):
        return pltpu.make_async_remote_copy(
            src_ref=src.at[peer], dst_ref=dst.at[mine], send_sem=send.at[peer], recv_sem=recv.at[mine],
            device_id=(peer, tm), device_id_type=MESH,
        )

    def give_back(c, peer, mine):
        return pltpu.make_async_remote_copy(
            src_ref=sub_out.at[c, peer], dst_ref=back_ref.at[c, mine],
            send_sem=back_send.at[c, peer], recv_sem=back_recv.at[c, mine],
            device_id=(peer, tm), device_id_type=MESH,
        )

    def ring(way, step, c):
        shard = lax.rem(tm - step + group, group) if way == 0 else lax.rem(tm + step, group)
        src = model_ref.at[c] if step == 0 else panel.at[shard, c]
        return pltpu.make_async_remote_copy(
            src_ref=src, dst_ref=panel.at[shard, c],
            send_sem=ring_send.at[way, step, c], recv_sem=ring_recv.at[way, step, c],
            device_id=(me, right if way == 0 else left), device_id_type=MESH,
        )

    hops = (group // 2, (group - 1) // 2)

    def arrived(way, step, c):
        shard = lax.rem(tm - step - 1 + group, group) if way == 0 else lax.rem(tm + step + 1, group)
        return pltpu.make_async_remote_copy(
            src_ref=panel.at[shard, c], dst_ref=panel.at[shard, c],
            send_sem=ring_send.at[way, step, c], recv_sem=ring_recv.at[way, step, c],
            device_id=(me, right if way == 0 else left), device_id_type=MESH,
        ), shard

    for c in range(2):
        for way in range(2):
            if hops[way] > 0:
                ring(way, 0, c).start()

    @pl.loop(1, tiles)
    def _(k):
        to_tile(req_ref, asked, ask_send, ask_recv, lax.rem(me + k, tiles), me).start()

    asked[me] = req_ref[me]

    def spread(c, shard, values):
        for h in range(shard_rows // 16):
            for t in range(values.shape[1] // sub_cols):
                cells[c, shard * (shard_rows // 16) + h, t] = values[
                    h * 16 : (h + 1) * 16, t * sub_cols : (t + 1) * sub_cols
                ]

    for c in range(2):
        spread(c, tm, model_ref[c])
    for step in range(hops[0]):
        for c in range(2):
            for way in range(2):
                if step < hops[way]:
                    copy, shard = arrived(way, step, c)
                    copy.wait_recv()
                    if step + 1 < hops[way]:
                        ring(way, step + 1, c).start()
                    spread(c, shard, panel[shard, c])

    @pl.loop(1, tiles)
    def _(k):
        peer = lax.rem(me + k, tiles)
        to_tile(asked, asked, ask_send, ask_recv, peer, peer).wait_recv()

    to_smem = pltpu.make_async_copy(asked, asked_s, smem_sem)
    to_smem.start()
    to_smem.wait()

    tall, broad = sub_rows + 16, 2 * sub_cols
    row_gap = lax.broadcasted_iota(jnp.int32, (sub_rows, tall), 1) - lax.broadcasted_iota(
        jnp.int32, (sub_rows, tall), 0
    )
    col_gap = lax.broadcasted_iota(jnp.int32, (broad, sub_cols), 0) - lax.broadcasted_iota(
        jnp.int32, (broad, sub_cols), 1
    )

    def cut(peer, target):
        for s in range(slots):
            row = jnp.maximum(asked_s[peer, 0, 2 * s], 0)
            col = jnp.maximum(asked_s[peer, 0, 2 * s + 1], 0)
            top = jnp.minimum(lax.div(row, 16), cells.shape[1] - tall // 16)
            base = jnp.minimum(lax.div(col, sub_cols), cells.shape[2] - 2)
            window = jnp.concatenate(
                [
                    jnp.concatenate([cells[c, top + i, base + j] for c in range(2) for j in range(2)], axis=1)
                    for i in range(tall // 16)
                ],
                axis=0,
            )
            pick_rows = (row_gap == row - 16 * top).astype(jnp.float32).astype(jnp.bfloat16)
            pick_cols = (col_gap == col - sub_cols * base).astype(jnp.float32).astype(jnp.bfloat16)
            window = jnp.dot(pick_rows, window, preferred_element_type=jnp.float32).astype(jnp.bfloat16)
            window = jnp.concatenate([window[:, :broad], window[:, broad:]], axis=0)
            window = jnp.dot(window, pick_cols, preferred_element_type=jnp.float32).astype(jnp.bfloat16)
            target[peer, s] = window.reshape(2, sub_rows, sub_cols)

    @pl.loop(0, (tiles - 1) // width)
    def _(i):
        peers = [lax.rem(me + 1 + i * width + w, tiles) for w in range(width)]
        for peer in peers:
            cut(peer, patch_out)
        for peer in peers:
            to_tile(patch_out, patch_in, patch_send, patch_recv, peer, me).start()

    cut(me, patch_in)
    for load in loads:
        load.wait()

    def work(peer, target):
        for s in range(slots):
            b = inv_ref[peer * slots + s]
            patch = patch_in[peer, s].reshape(2 * sub_rows, sub_cols)
            cols = cols_ref[b]
            sampled = jnp.dot(patch, cols, preferred_element_type=jnp.float32)
            weights = rows_ref[b].astype(jnp.float32)
            sampled = sampled.reshape(2, sub_rows, vis_n)
            predicted = jnp.sum(weights[None] * sampled, axis=1)
            residual = vis_ref[b].astype(jnp.float32) - predicted
            res_slots[peer * slots + s] = residual
            weighted = (weights[None] * residual[:, None, :]).astype(jnp.bfloat16)
            weighted = weighted.reshape(2 * sub_rows, vis_n)
            sub = lax.dot_general(
                weighted, cols, (((1,), (1,)), ((), ())), preferred_element_type=jnp.float32
            )
            sub = sub.astype(jnp.bfloat16).reshape(2, sub_rows, sub_cols)
            for c in range(2):
                target[c, peer, s] = sub[c]

    work(me, back_ref)
    acc[...] = jnp.zeros_like(acc)

    @pl.loop(0, (tiles - 1) // width)
    def _(i):
        peers = [lax.rem(me + tiles - 1 - i * width - w, tiles) for w in range(width)]
        for peer in peers:
            to_tile(patch_out, patch_in, patch_send, patch_recv, peer, peer).wait_recv()
        for peer in peers:
            work(peer, sub_out)
        for peer in peers:
            give_back(0, peer, me).start()

    @pl.loop(1, tiles)
    def _(k):
        give_back(1, lax.rem(me + tiles - k, tiles), me).start()

    @pl.loop(0, res_ref.shape[0], unroll=4)
    def _(b):
        res_ref[b] = res_slots[pos_ref[b]]

    chunk = acc.shape[3]
    halves = acc.shape[1]
    tile_rows = acc.shape[2]

    def sum_copy(c, h, way, step):
        length = hops[way ^ h]
        away = length - step
        shard = lax.rem(tm - away + group, group) if way == 0 else lax.rem(tm + away, group)
        rows = pl.ds(pl.multiple_of(shard * shard_rows, shard_rows), shard_rows)
        src = acc.at[c, h, rows] if step == 0 else sums.at[c, h, way, step - 1]
        copy = pltpu.make_async_remote_copy(
            src_ref=src, dst_ref=sums.at[c, h, way, step],
            send_sem=sum_send.at[c, h, way, step], recv_sem=sum_recv.at[c, h, way, step],
            device_id=(me, left if way == 0 else right), device_id_type=MESH,
        )
        return copy, rows

    chains = [(h, way) for h in range(halves) for way in range(2) if hops[way ^ h] > 0]

    def sum_step(c, step):
        for h, way in chains:
            length = hops[way ^ h]
            if step > 0 and step <= length:
                sum_copy(c, h, way, step - 1)[0].wait_recv()
            if step < length:
                copy, rows = sum_copy(c, h, way, step)
                if step > 0:
                    sums[c, h, way, step - 1] += acc[c, h, rows]
                copy.start()
        if step == max(hops):
            own = pl.ds(pl.multiple_of(tm * shard_rows, shard_rows), shard_rows)
            for h in range(halves):
                total = acc[c, h, own]
                for way in range(2):
                    if hops[way ^ h] > 0:
                        total += sums[c, h, way, hops[way ^ h] - 1]
                out_ref[c, :, h * chunk : (h + 1) * chunk] = total

    batch = min(8, tiles)
    turns = tiles // batch
    lane = lax.broadcasted_iota(jnp.int32, (1, 128), 1)
    grid_row = lax.broadcasted_iota(jnp.int32, (tile_rows, 128), 0)
    place_gap = lax.broadcasted_iota(jnp.int32, (sub_cols, broad), 1) - lax.broadcasted_iota(
        jnp.int32, (sub_cols, broad), 0
    )
    per = 128 // sub_rows
    col_tiles = spread_ref.shape[1] // sub_cols

    def add_batch(c, i):
        starts = []
        for w in range(batch):
            k = i * batch + w
            peer = lax.rem(me + k, tiles)

            @pl.when(k > 0)
            def _():
                give_back(c, peer, peer).wait_recv()

        for w in range(batch):
            peer = lax.rem(me + i * batch + w, tiles)
            for s in range(slots):
                row = asked_s[peer, 0, 2 * s]
                col = jnp.maximum(asked_s[peer, 0, 2 * s + 1], 0)
                starts.append(jnp.where(row < 0, -4 * tile_rows, row))
                base = jnp.minimum(lax.div(col, sub_cols), col_tiles - 2)
                put = (place_gap == col - sub_cols * base).astype(jnp.float32).astype(jnp.bfloat16)
                moved = jnp.dot(back_ref[c, peer, s], put, preferred_element_type=jnp.float32)
                at = (w * slots + s) * sub_rows
                where = jnp.broadcast_to(base, (sub_rows, sub_cols))
                low, high = moved[:, :sub_cols], moved[:, sub_cols:]
                for t in range(col_tiles):
                    piece = jnp.where(where == t, low, jnp.where(where == t - 1, high, 0.0))
                    spread_ref[at : at + sub_rows, t * sub_cols : (t + 1) * sub_cols] = piece.astype(jnp.bfloat16)
        hot = []
        for q in range(0, len(starts), per):
            first = jnp.broadcast_to(starts[q + per - 1], (1, 128))
            for r in range(per - 2, -1, -1):
                first = jnp.where(lane < (r + 1) * sub_rows, starts[q + r], first)
            first = first + lax.rem(lane, sub_rows)
            hot.append((grid_row == first).astype(jnp.float32).astype(jnp.bfloat16))
        hot = jnp.concatenate(hot, axis=1)
        for h in range(halves):
            for n in range(0, chunk, 256):
                at = h * chunk + n
                acc[c, h, :, n : n + 256] += jnp.dot(
                    hot, spread_ref[:, at : at + 256], preferred_element_type=jnp.float32
                )

    @pl.loop(0, 2 * turns)
    def _(j):
        add_batch(j // turns, lax.rem(j, turns))
        for step in range(max(hops)):

            @pl.when(j == turns - 1 + step * turns // max(hops))
            def _():
                sum_step(0, step)

    sum_step(1, 0)
    sum_step(0, max(hops))
    for step in range(max(hops)):
        sum_step(1, step + 1)

    for c in range(2):
        for way in range(2):
            for step in range(hops[way]):
                ring(way, step, c).wait_send()
        for h, way in chains:
            for step in range(hops[way ^ h]):
                sum_copy(c, h, way, step)[0].wait_send()

    @pl.loop(1, tiles)
    def _(k):
        peer = lax.rem(me + k, tiles)
        to_tile(req_ref, asked, ask_send, ask_recv, peer, me).wait_send()
        to_tile(patch_out, patch_in, patch_send, patch_recv, peer, me).wait_send()
        for c in range(2):
            give_back(c, peer, me).wait_send()


def smem():
    return pl.BlockSpec(memory_space=pltpu.SMEM)


def vmem():
    return pl.BlockSpec(memory_space=pltpu.VMEM)


def anywhere():
    return pl.BlockSpec(memory_space=pl.ANY)


def shards(model, kern_rows, kern_cols, visibilities, owner_tile, row_offset, col_offset):
    tiles = lax.axis_size("tile")
    group = lax.axis_size("tm")
    blocks = owner_tile.shape[0]
    slots = (blocks + tiles - 1) // tiles + 1
    sub_rows = kern_rows.shape[1]
    sub_cols = kern_cols.shape[1]
    vis_n = kern_rows.shape[2]
    shard_rows, grid_cols = model.shape[1:]
    tile_rows = group * shard_rows

    owners = owner_tile[:, 0]
    ids = jnp.arange(blocks, dtype=jnp.int32)
    earlier = (owners[:, None] == owners[None, :]) & (ids[None, :] < ids[:, None])
    place = owners * slots + jnp.sum(earlier.astype(jnp.int32), axis=1)
    hot = (place[None, :] == jnp.arange(tiles * slots, dtype=jnp.int32)[:, None]).astype(jnp.int32)
    inverse = jnp.sum(hot * ids[None, :], axis=1)
    wanted = jnp.stack([row_offset, col_offset], axis=0)
    request = (jnp.sum(hot[:, None, :] * (wanted + 1)[None], axis=2) - 1).reshape(tiles, 1, slots * 2)
    request = jnp.pad(request, ((0, 0), (0, 0), (0, 128 - slots * 2)))

    pair = (tiles, slots, 2, sub_rows, sub_cols)
    hops = max(group // 2, 1)
    dma = pltpu.SemaphoreType.DMA
    back = (2, tiles, slots, sub_rows, sub_cols)
    batch = min(8, tiles)
    return pl.pallas_call(
        functools.partial(major_kernel, tiles, group, slots),
        out_shape=[
            jax.ShapeDtypeStruct((2, shard_rows, grid_cols), jnp.float32),
            jax.ShapeDtypeStruct((blocks, 2, vis_n), jnp.float32),
        ],
        in_specs=[smem(), smem(), vmem(), vmem(), anywhere(), anywhere(), anywhere()],
        out_specs=[vmem(), vmem()],
        scratch_shapes=[
            pltpu.VMEM((tiles, 1, 128), jnp.int32),
            pltpu.VMEM((group, 2, shard_rows, grid_cols), jnp.bfloat16),
            pltpu.VMEM((2, tile_rows // 16, grid_cols // sub_cols, 16, sub_cols), jnp.bfloat16),
            pltpu.SMEM((tiles, 1, 128), jnp.int32),
            pltpu.VMEM(pair, jnp.bfloat16),
            pltpu.VMEM(pair, jnp.bfloat16),
            pltpu.VMEM(back, jnp.bfloat16),
            pltpu.VMEM(back, jnp.bfloat16),
            pltpu.VMEM(kern_rows.shape, jnp.bfloat16),
            pltpu.VMEM(kern_cols.shape, jnp.bfloat16),
            pltpu.VMEM(visibilities.shape, jnp.bfloat16),
            pltpu.VMEM((tiles * slots, 2, vis_n), jnp.float32),
            pltpu.VMEM((batch * slots * sub_rows, grid_cols), jnp.bfloat16),
            pltpu.VMEM((2, 2, tile_rows, grid_cols // 2), jnp.float32),
            pltpu.VMEM((2, 2, 2, hops, shard_rows, grid_cols // 2), jnp.float32),
            dma((3,)),
            dma,
            dma((tiles,)),
            dma((tiles,)),
            dma((2, hops, 2)),
            dma((2, hops, 2)),
            dma((tiles,)),
            dma((tiles,)),
            dma((2, tiles)),
            dma((2, tiles)),
            dma((2, 2, 2, hops)),
            dma((2, 2, 2, hops)),
        ],
        compiler_params=pltpu.CompilerParams(
            collective_id=0, has_side_effects=True, vmem_limit_bytes=VMEM_LIMIT
        ),
        name="major",
    )(inverse, place, request, model, kern_rows, kern_cols, visibilities)


def solution(mesh):
    placed = (
        P(None, ("tile", "tm"), None),
        P(("tile", "tm"), None, None),
        P(("tile", "tm"), None, None),
        P(("tile", "tm"), None, None),
        P(("tile", "tm"), None),
        P(("tile", "tm")),
        P(("tile", "tm")),
    )
    return jax.shard_map(
        shards,
        mesh=mesh,
        in_specs=placed,
        out_specs=(P(None, ("tile", "tm"), None), P(("tile", "tm"), None, None)),
        check_vma=False,
    )
```

```python
import functools

import jax
import jax.numpy as jnp
from jax import lax
from jax.experimental import pallas as pl
from jax.experimental.pallas import tpu as pltpu
from jax.sharding import PartitionSpec as P

VMEM_LIMIT = 48 * 1024 * 1024
MESH = pl.DeviceIdType.MESH


def tile_dims(tiles):
    return 8, (2 if tiles >= 16 else 1)


def major_kernel(
    tiles, group, slots,
    inv_ref, pos_ref, req_ref, model_ref, rows_hbm, cols_hbm, vis_hbm,
    out_ref, res_ref,
    asked, swapped, panel, cells, asked_s, patch_out, patch_in, sub_out, back_ref, rows_ref, cols_ref, vis_ref, res_slots,
    spread_ref, acc, sums, gift,
    kern_sem, smem_sem, ask_send, ask_recv, swap_send, swap_recv, strip_send, strip_recv, patch_send, patch_recv, back_send, back_recv,
    sum_send, sum_recv,
):
    me = lax.axis_index("tile")
    tm = lax.axis_index("tm")
    sub_rows, sub_cols = patch_in.shape[3], patch_in.shape[4]
    shard_rows = model_ref.shape[1]
    vis_n = rows_ref.shape[2]
    depth, cores = tile_dims(tiles)
    kind = lax.rem(tm // 2, 2)
    turn = 2 * lax.rem(tm, 2) - 1

    def plane(start, offset):
        return lax.rem(start + offset + group, group)

    mate, across, far = plane(tm, -turn), plane(tm, turn), plane(tm, 3 * turn)
    skip_to, skip_from = plane(tm, -2 * turn), plane(tm, 2 * turn)
    passed = (far, across, skip_from)
    mates = (plane(mate, -3 * turn), plane(mate, -turn), plane(mate, -2 * turn))
    x, z, core = me // (depth * cores), lax.rem(me // cores, depth), lax.rem(me, cores)
    opposite = (x * depth + lax.rem(z + depth // 2, depth)) * cores + core
    per_z = tiles // depth
    near = depth // 2 + 1
    own = (near // 2) * per_z

    def partner(i, flip=False):
        k = lax.rem(own + i, tiles)
        other = k // (near * per_z)
        rest = k - other * near * per_z
        dz, dx, dc = rest // per_z, lax.rem(rest, per_z) // cores, lax.rem(rest, cores)
        back_dz, back_dx = near - 1 - 2 * other - dz, lax.rem(per_z // cores - dx, per_z // cores)
        back = other * near * per_z + back_dz * per_z + back_dx * cores + dc
        if flip:
            dz, dx, k, back = back_dz, back_dx, back, k
        there = (
            lax.rem(x + dx, per_z // cores) * depth + lax.rem(z + dz - near // 2 + other + depth, depth)
        ) * cores + lax.rem(core + dc, cores)
        return (there, jnp.where(other == 1, across, tm)), k, back

    width = 3 if (tiles - 1) % 3 == 0 else 1

    loads = [
        pltpu.make_async_copy(src, dst, kern_sem.at[i])
        for i, (src, dst) in enumerate(((rows_hbm, rows_ref), (cols_hbm, cols_ref), (vis_hbm, vis_ref)))
    ]
    for load in loads:
        load.start()

    barrier = pltpu.get_barrier_semaphore()

    @pl.loop(1, tiles)
    def _(i):
        pl.semaphore_signal(barrier, inc=1, device_id=partner(i)[0], device_id_type=MESH)

    others = ((me, mate), (me, far), (me, skip_to), (me, skip_from), (opposite, tm))
    for other in others:
        pl.semaphore_signal(barrier, inc=1, device_id=other, device_id_type=MESH)
    pl.semaphore_wait(barrier, tiles - 1 + len(others))

    def to_tile(src, dst, send, recv, i):
        device, here, there = partner(i)
        return pltpu.make_async_remote_copy(
            src_ref=src.at[here], dst_ref=dst.at[there], send_sem=send.at[here], recv_sem=recv.at[there],
            device_id=device, device_id_type=MESH,
        )

    def from_tile(dst, send, recv, i):
        device, here, there = partner(i, True)
        return pltpu.make_async_remote_copy(
            src_ref=dst.at[here], dst_ref=dst.at[here], send_sem=send.at[here], recv_sem=recv.at[here],
            device_id=device, device_id_type=MESH,
        )

    def give_back(c, i):
        device, here, there = partner(i, True)
        return pltpu.make_async_remote_copy(
            src_ref=sub_out.at[c, here], dst_ref=back_ref.at[c, there],
            send_sem=back_send.at[c, here], recv_sem=back_recv.at[c, there],
            device_id=device, device_id_type=MESH,
        )

    def returned(c, i):
        device, here, there = partner(i)
        return pltpu.make_async_remote_copy(
            src_ref=back_ref.at[c, here], dst_ref=back_ref.at[c, here],
            send_sem=back_send.at[c, here], recv_sem=back_recv.at[c, here],
            device_id=device, device_id_type=MESH,
        )

    def swap(c):
        return pltpu.make_async_remote_copy(
            src_ref=model_ref.at[c], dst_ref=swapped.at[c], send_sem=swap_send.at[c], recv_sem=swap_recv.at[c],
            device_id=(opposite, tm), device_id_type=MESH,
        )

    def strip(src, index, label, shard, c, to):
        return pltpu.make_async_remote_copy(
            src_ref=src, dst_ref=panel.at[shard, c],
            send_sem=strip_send.at[index, c], recv_sem=strip_recv.at[label, c],
            device_id=(me, to), device_id_type=MESH,
        )

    def outgoing(index, c):
        src = model_ref.at[c] if index < 2 else swapped.at[c]
        same = kind == (0 if index < 2 else 1)
        step = index % 2
        label = jnp.where(same, step, 2 + step)
        to = jnp.where(same, (mate, far)[step], (across, skip_to)[step])
        return strip(src, index, label, tm, c, to)

    def passing(f, c):
        return strip(panel.at[passed[f], c], 4 + f, 4 + f, passed[f], c, mate)

    for c in range(2):
        swap(c).start()
        for index in range(2):
            outgoing(index, c).start()

    @pl.loop(1, tiles)
    def _(i):
        to_tile(req_ref, asked, ask_send, ask_recv, i).start()

    asked[own] = req_ref[own]

    def spread(c, shard, values):
        for h in range(shard_rows // 16):
            for t in range(values.shape[1] // sub_cols):
                cells[c, shard * (shard_rows // 16) + h, t] = values[
                    h * 16 : (h + 1) * 16, t * sub_cols : (t + 1) * sub_cols
                ]

    for c in range(2):
        swap(c).wait_recv()
        for index in range(2, 4):
            outgoing(index, c).start()
    for c in range(2):
        spread(c, tm, jnp.where(kind == 0, model_ref[c], swapped[c]))
    for c in range(2):
        for f in range(3):
            strip(panel.at[passed[f], c], 4 + f, 1 + f, passed[f], c, mate).wait_recv()
            passing(f, c).start()
            spread(c, passed[f], panel[passed[f], c])
    for c in range(2):
        strip(panel.at[mate, c], 0, 0, mate, c, mate).wait_recv()
        spread(c, mate, panel[mate, c])
        for f in range(3):
            strip(panel.at[mates[f], c], 4 + f, 4 + f, mates[f], c, mate).wait_recv()
            spread(c, mates[f], panel[mates[f], c])

    @pl.loop(1, tiles)
    def _(i):
        from_tile(asked, ask_send, ask_recv, i).wait_recv()

    to_smem = pltpu.make_async_copy(asked, asked_s, smem_sem)
    to_smem.start()
    to_smem.wait()

    tall, broad = sub_rows + 16, 2 * sub_cols
    row_gap = lax.broadcasted_iota(jnp.int32, (sub_rows, tall), 1) - lax.broadcasted_iota(
        jnp.int32, (sub_rows, tall), 0
    )
    col_gap = lax.broadcasted_iota(jnp.int32, (broad, sub_cols), 0) - lax.broadcasted_iota(
        jnp.int32, (broad, sub_cols), 1
    )

    def cut(peer, target):
        for s in range(slots):
            row = jnp.maximum(asked_s[peer, 0, 2 * s], 0)
            col = jnp.maximum(asked_s[peer, 0, 2 * s + 1], 0)
            top = jnp.minimum(lax.div(row, 16), cells.shape[1] - tall // 16)
            base = jnp.minimum(lax.div(col, sub_cols), cells.shape[2] - 2)
            window = jnp.concatenate(
                [
                    jnp.concatenate([cells[c, top + i, base + j] for c in range(2) for j in range(2)], axis=1)
                    for i in range(tall // 16)
                ],
                axis=0,
            )
            pick_rows = (row_gap == row - 16 * top).astype(jnp.float32).astype(jnp.bfloat16)
            pick_cols = (col_gap == col - sub_cols * base).astype(jnp.float32).astype(jnp.bfloat16)
            window = jnp.dot(pick_rows, window, preferred_element_type=jnp.float32).astype(jnp.bfloat16)
            window = jnp.concatenate([window[:, :broad], window[:, broad:]], axis=0)
            window = jnp.dot(window, pick_cols, preferred_element_type=jnp.float32).astype(jnp.bfloat16)
            target[peer, s] = window.reshape(2, sub_rows, sub_cols)

    @pl.loop(0, (tiles - 1) // width)
    def _(i):
        turns_here = [1 + i * width + w for w in range(width)]
        for t in turns_here:
            cut(partner(t)[1], patch_out)
        for t in turns_here:
            to_tile(patch_out, patch_in, patch_send, patch_recv, t).start()

    cut(own, patch_in)
    for load in loads:
        load.wait()

    def work(peer, target):
        for s in range(slots):
            b = inv_ref[peer * slots + s]
            patch = patch_in[peer, s].reshape(2 * sub_rows, sub_cols)
            cols = cols_ref[b]
            sampled = jnp.dot(patch, cols, preferred_element_type=jnp.float32)
            weights = rows_ref[b].astype(jnp.float32)
            sampled = sampled.reshape(2, sub_rows, vis_n)
            predicted = jnp.sum(weights[None] * sampled, axis=1)
            residual = vis_ref[b].astype(jnp.float32) - predicted
            res_slots[peer * slots + s] = residual
            weighted = (weights[None] * residual[:, None, :]).astype(jnp.bfloat16)
            weighted = weighted.reshape(2 * sub_rows, vis_n)
            sub = lax.dot_general(
                weighted, cols, (((1,), (1,)), ((), ())), preferred_element_type=jnp.float32
            )
            sub = sub.astype(jnp.bfloat16).reshape(2, sub_rows, sub_cols)
            for c in range(2):
                target[c, peer, s] = sub[c]

    work(own, back_ref)
    acc[...] = jnp.zeros_like(acc)

    @pl.loop(0, (tiles - 1) // width)
    def _(i):
        turns_here = [1 + i * width + w for w in range(width)]
        for t in turns_here:
            from_tile(patch_in, patch_send, patch_recv, t).wait_recv()
        for t in turns_here:
            work(partner(t, True)[1], sub_out)
        for t in turns_here:
            give_back(0, t).start()

    @pl.loop(1, tiles)
    def _(i):
        give_back(1, i).start()

    @pl.loop(0, res_ref.shape[0], unroll=4)
    def _(b):
        res_ref[b] = res_slots[pos_ref[b]]

    chunk = acc.shape[3]
    halves = acc.shape[1]
    tile_rows = acc.shape[2]

    def rows_of(shard):
        return pl.ds(pl.multiple_of(shard * shard_rows, shard_rows), shard_rows)

    def sum_copy(c, h, index):
        if index in (0, 4, 5, 6):
            src, device = acc.at[c, h, rows_of(mate if index == 0 else mates[index - 4])], (me, mate)
        elif index < 4:
            src, device = sums.at[c, h, 3 + index], (me, passed[index - 1])
        else:
            src, device = gift.at[c, h], (opposite, tm)
        return pltpu.make_async_remote_copy(
            src_ref=src, dst_ref=sums.at[c, h, index],
            send_sem=sum_send.at[c, h, index], recv_sem=sum_recv.at[c, h, index],
            device_id=device, device_id_type=MESH,
        )

    def sum_step(c, step):
        for h in range(halves):
            cols = slice(h * chunk, (h + 1) * chunk)
            if step == 0:
                for index in (4, 5, 6, 0):
                    sum_copy(c, h, index).start()
            elif step == 1:
                for f in range(3):
                    sum_copy(c, h, 4 + f).wait_recv()
                    sums[c, h, 4 + f] += acc[c, h, rows_of(passed[f])]
                    sum_copy(c, h, 1 + f).start()
            elif step == 2:
                for index in range(4):
                    sum_copy(c, h, index).wait_recv()
                alike = acc[c, h, rows_of(tm)] + sums[c, h, 0] + sums[c, h, 1]
                unlike = sums[c, h, 2] + sums[c, h, 3]
                gift[c, h] = jnp.where(kind == 0, unlike, alike)
                sum_copy(c, h, 7).start()
                out_ref[c, :, cols] = jnp.where(kind == 0, alike, unlike)
            else:
                sum_copy(c, h, 7).wait_recv()
                out_ref[c, :, cols] += sums[c, h, 7]

    batch = min(8, tiles)
    turns = tiles // batch
    lane = lax.broadcasted_iota(jnp.int32, (1, 128), 1)
    grid_row = lax.broadcasted_iota(jnp.int32, (tile_rows, 128), 0)
    place_gap = lax.broadcasted_iota(jnp.int32, (sub_cols, broad), 1) - lax.broadcasted_iota(
        jnp.int32, (sub_cols, broad), 0
    )
    per = 128 // sub_rows
    col_tiles = spread_ref.shape[1] // sub_cols

    def add_batch(c, i):
        starts = []
        for w in range(batch):
            t = i * batch + w

            @pl.when(t > 0)
            def _():
                returned(c, t).wait_recv()

        for w in range(batch):
            peer = partner(i * batch + w)[1]
            for s in range(slots):
                row = asked_s[peer, 0, 2 * s]
                col = jnp.maximum(asked_s[peer, 0, 2 * s + 1], 0)
                starts.append(jnp.where(row < 0, -4 * tile_rows, row))
                base = jnp.minimum(lax.div(col, sub_cols), col_tiles - 2)
                put = (place_gap == col - sub_cols * base).astype(jnp.float32).astype(jnp.bfloat16)
                moved = jnp.dot(back_ref[c, peer, s], put, preferred_element_type=jnp.float32)
                at = (w * slots + s) * sub_rows
                where = jnp.broadcast_to(base, (sub_rows, sub_cols))
                low, high = moved[:, :sub_cols], moved[:, sub_cols:]
                for t in range(col_tiles):
                    piece = jnp.where(where == t, low, jnp.where(where == t - 1, high, 0.0))
                    spread_ref[at : at + sub_rows, t * sub_cols : (t + 1) * sub_cols] = piece.astype(jnp.bfloat16)
        hot = []
        for q in range(0, len(starts), per):
            first = jnp.broadcast_to(starts[q + per - 1], (1, 128))
            for r in range(per - 2, -1, -1):
                first = jnp.where(lane < (r + 1) * sub_rows, starts[q + r], first)
            first = first + lax.rem(lane, sub_rows)
            hot.append((grid_row == first).astype(jnp.float32).astype(jnp.bfloat16))
        hot = jnp.concatenate(hot, axis=1)
        for h in range(halves):
            for n in range(0, chunk, 256):
                at = h * chunk + n
                acc[c, h, :, n : n + 256] += jnp.dot(
                    hot, spread_ref[:, at : at + 256], preferred_element_type=jnp.float32
                )

    @pl.loop(0, 2 * turns)
    def _(j):
        add_batch(j // turns, lax.rem(j, turns))
        for step in range(4):

            @pl.when(j == turns - 1 + step * turns // 4)
            def _():
                sum_step(0, step)

    for step in range(4):
        sum_step(1, step)

    for c in range(2):
        swap(c).wait_send()
        for index in range(4):
            outgoing(index, c).wait_send()
        for f in range(3):
            passing(f, c).wait_send()
        for h in range(halves):
            for index in range(8):
                sum_copy(c, h, index).wait_send()

    @pl.loop(1, tiles)
    def _(i):
        to_tile(req_ref, asked, ask_send, ask_recv, i).wait_send()
        to_tile(patch_out, patch_in, patch_send, patch_recv, i).wait_send()
        for c in range(2):
            give_back(c, i).wait_send()


def smem():
    return pl.BlockSpec(memory_space=pltpu.SMEM)


def vmem():
    return pl.BlockSpec(memory_space=pltpu.VMEM)


def anywhere():
    return pl.BlockSpec(memory_space=pl.ANY)


def shards(model, kern_rows, kern_cols, visibilities, owner_tile, row_offset, col_offset):
    tiles = lax.axis_size("tile")
    group = lax.axis_size("tm")
    blocks = owner_tile.shape[0]
    slots = (blocks + tiles - 1) // tiles + 1
    sub_rows = kern_rows.shape[1]
    sub_cols = kern_cols.shape[1]
    vis_n = kern_rows.shape[2]
    shard_rows, grid_cols = model.shape[1:]
    tile_rows = group * shard_rows

    owners = owner_tile[:, 0]
    ids = jnp.arange(blocks, dtype=jnp.int32)
    earlier = (owners[:, None] == owners[None, :]) & (ids[None, :] < ids[:, None])
    depth, cores = tile_dims(tiles)
    near = depth // 2 + 1
    per_z = tiles // depth
    me = lax.axis_index("tile")
    kind = lax.rem(lax.axis_index("tm") // 2, 2)
    to_x = lax.rem(owners // (depth * cores) - me // (depth * cores) + per_z, per_z // cores)
    to_core = lax.rem(lax.rem(owners, cores) - lax.rem(me, cores) + cores, cores)
    to_z = lax.rem(
        lax.rem(owners // cores, depth) - lax.rem(me // cores, depth) + near // 2 + (4 - kind) * (depth // 2), depth
    )
    other = (to_z >= near).astype(jnp.int32)
    to_z = to_z - other * near
    at = (other * near + to_z) * per_z + to_x * cores + to_core
    place = at * slots + jnp.sum(earlier.astype(jnp.int32), axis=1)
    hot = (place[None, :] == jnp.arange(tiles * slots, dtype=jnp.int32)[:, None]).astype(jnp.int32)
    inverse = jnp.sum(hot * ids[None, :], axis=1)
    wanted = jnp.stack([row_offset, col_offset], axis=0)
    request = (jnp.sum(hot[:, None, :] * (wanted + 1)[None], axis=2) - 1).reshape(tiles, 1, slots * 2)
    request = jnp.pad(request, ((0, 0), (0, 0), (0, 128 - slots * 2)))

    pair = (tiles, slots, 2, sub_rows, sub_cols)
    dma = pltpu.SemaphoreType.DMA
    back = (2, tiles, slots, sub_rows, sub_cols)
    batch = min(8, tiles)
    return pl.pallas_call(
        functools.partial(major_kernel, tiles, group, slots),
        out_shape=[
            jax.ShapeDtypeStruct((2, shard_rows, grid_cols), jnp.float32),
            jax.ShapeDtypeStruct((blocks, 2, vis_n), jnp.float32),
        ],
        in_specs=[smem(), smem(), vmem(), vmem(), anywhere(), anywhere(), anywhere()],
        out_specs=[vmem(), vmem()],
        scratch_shapes=[
            pltpu.VMEM((tiles, 1, 128), jnp.int32),
            pltpu.VMEM((2, shard_rows, grid_cols), jnp.bfloat16),
            pltpu.VMEM((group, 2, shard_rows, grid_cols), jnp.bfloat16),
            pltpu.VMEM((2, tile_rows // 16, grid_cols // sub_cols, 16, sub_cols), jnp.bfloat16),
            pltpu.SMEM((tiles, 1, 128), jnp.int32),
            pltpu.VMEM(pair, jnp.bfloat16),
            pltpu.VMEM(pair, jnp.bfloat16),
            pltpu.VMEM(back, jnp.bfloat16),
            pltpu.VMEM(back, jnp.bfloat16),
            pltpu.VMEM(kern_rows.shape, jnp.bfloat16),
            pltpu.VMEM(kern_cols.shape, jnp.bfloat16),
            pltpu.VMEM(visibilities.shape, jnp.bfloat16),
            pltpu.VMEM((tiles * slots, 2, vis_n), jnp.float32),
            pltpu.VMEM((batch * slots * sub_rows, grid_cols), jnp.bfloat16),
            pltpu.VMEM((2, 2, tile_rows, grid_cols // 2), jnp.float32),
            pltpu.VMEM((2, 2, 8, shard_rows, grid_cols // 2), jnp.float32),
            pltpu.VMEM((2, 2, shard_rows, grid_cols // 2), jnp.float32),
            dma((3,)),
            dma,
            dma((tiles,)),
            dma((tiles,)),
            dma((2,)),
            dma((2,)),
            dma((7, 2)),
            dma((7, 2)),
            dma((tiles,)),
            dma((tiles,)),
            dma((2, tiles)),
            dma((2, tiles)),
            dma((2, 2, 8)),
            dma((2, 2, 8)),
        ],
        compiler_params=pltpu.CompilerParams(
            collective_id=0, has_side_effects=True, vmem_limit_bytes=VMEM_LIMIT
        ),
        name="major",
    )(inverse, place, request, model, kern_rows, kern_cols, visibilities)


def solution(mesh):
    placed = (
        P(None, ("tile", "tm"), None),
        P(("tile", "tm"), None, None),
        P(("tile", "tm"), None, None),
        P(("tile", "tm"), None, None),
        P(("tile", "tm"), None),
        P(("tile", "tm")),
        P(("tile", "tm")),
    )
    return jax.shard_map(
        shards,
        mesh=mesh,
        in_specs=placed,
        out_specs=(P(None, ("tile", "tm"), None), P(("tile", "tm"), None, None)),
        check_vma=False,
    )
```

```python
import functools

import jax
import jax.numpy as jnp
from jax import lax
from jax.experimental import pallas as pl
from jax.experimental.pallas import tpu as pltpu
from jax.sharding import PartitionSpec as P

VMEM_LIMIT = 63 * 1024 * 1024
MESH = pl.DeviceIdType.MESH


def major_kernel(
    tiles, group, slots,
    owner_hbm, row_hbm, col_hbm, model_hbm, rows_hbm, cols_hbm, vis_hbm,
    out_ref, res_ref,
    wanted, model_ref, req_ref, pos_v, req_s, pos_s, asked, panel, cells, asked_s, patch_out, patch_in, sub_out, back_ref, rows_ref, cols_ref, vis_ref, res_slots,
    spread_ref, acc, sums,
    kern_sem, want_sem, smem_sem, ask_send, ask_recv, ring_send, ring_recv, patch_send, patch_recv, back_send, back_recv,
    sum_send, sum_recv,
):
    me = lax.axis_index("tile")
    tm = lax.axis_index("tm")
    blocks = res_ref.shape[0]
    sub_rows, sub_cols = patch_in.shape[3], patch_in.shape[4]
    shard_rows = model_ref.shape[1]
    vis_n = rows_ref.shape[2]
    right, left = lax.rem(tm + 1, group), lax.rem(tm + group - 1, group)
    width = 3 if (tiles - 1) % 3 == 0 else 1

    first = [
        pltpu.make_async_copy(src, dst, want_sem.at[i])
        for i, (src, dst) in enumerate(
            ((owner_hbm, wanted.at[0]), (row_hbm, wanted.at[1]), (col_hbm, wanted.at[2]), (model_hbm, model_ref))
        )
    ]
    for load in first:
        load.start()
    loads = [
        pltpu.make_async_copy(src, dst, kern_sem.at[i])
        for i, (src, dst) in enumerate(((rows_hbm, rows_ref), (cols_hbm, cols_ref), (vis_hbm, vis_ref)))
    ]
    for load in loads:
        load.start()

    barrier = pltpu.get_barrier_semaphore()

    @pl.loop(1, tiles)
    def _(k):
        pl.semaphore_signal(barrier, inc=1, device_id=(lax.rem(me + k, tiles), tm), device_id_type=MESH)

    near = [right, left] if group > 2 else [right]
    for other in near:
        pl.semaphore_signal(barrier, inc=1, device_id=(me, other), device_id_type=MESH)
    for load in first:
        load.wait()
    owner, row_at, col_at = wanted[0], wanted[1], wanted[2]
    ids = lax.broadcasted_iota(jnp.int32, (1, blocks), 1)
    down = lax.broadcasted_iota(jnp.int32, (blocks, blocks), 0)
    along = lax.broadcasted_iota(jnp.int32, (blocks, blocks), 1)
    owner_down = jnp.sum(jnp.where(down == along, owner, 0), axis=1, keepdims=True)
    earlier = jnp.where((owner_down == owner) & (down < along), 1, 0)
    place = owner * slots + jnp.sum(earlier, axis=0, keepdims=True)
    lanes = lax.broadcasted_iota(jnp.int32, (tiles, 128), 1)
    tile_at = lax.broadcasted_iota(jnp.int32, (tiles, blocks), 0) * slots
    request = jnp.zeros((tiles, 128), jnp.int32)
    for s in range(slots):
        hot = tile_at + s == place
        for lane_at, value in ((2 * s, row_at + 1), (2 * s + 1, col_at + 1), (2 * slots + s, ids + 1)):
            found = jnp.sum(jnp.where(hot, value, 0), axis=1, keepdims=True) - 1
            request = jnp.where(lanes == lane_at, found, request)
    req_ref[...] = request.reshape(tiles, 1, 128)
    pos_v[...] = jnp.concatenate([place, jnp.zeros((1, 128 - blocks), jnp.int32)], axis=1)
    lists = [
        pltpu.make_async_copy(src, dst, want_sem.at[4 + i])
        for i, (src, dst) in enumerate(((req_ref, req_s), (pos_v, pos_s)))
    ]
    for load in lists:
        load.start()
    pl.semaphore_wait(barrier, tiles - 1 + len(near))

    def to_tile(src, dst, send, recv, peer, mine):
        return pltpu.make_async_remote_copy(
            src_ref=src.at[peer], dst_ref=dst.at[mine], send_sem=send.at[peer], recv_sem=recv.at[mine],
            device_id=(peer, tm), device_id_type=MESH,
        )

    def give_back(c, peer, mine):
        return pltpu.make_async_remote_copy(
            src_ref=sub_out.at[c, peer], dst_ref=back_ref.at[c, mine],
            send_sem=back_send.at[c, peer], recv_sem=back_recv.at[c, mine],
            device_id=(peer, tm), device_id_type=MESH,
        )

    def ring(way, step, c):
        shard = lax.rem(tm - step + group, group) if way == 0 else lax.rem(tm + step, group)
        src = model_ref.at[c] if step == 0 else panel.at[shard, c]
        return pltpu.make_async_remote_copy(
            src_ref=src, dst_ref=panel.at[shard, c],
            send_sem=ring_send.at[way, step, c], recv_sem=ring_recv.at[way, step, c],
            device_id=(me, right if way == 0 else left), device_id_type=MESH,
        )

    hops = (group // 2, (group - 1) // 2)

    def arrived(way, step, c):
        shard = lax.rem(tm - step - 1 + group, group) if way == 0 else lax.rem(tm + step + 1, group)
        return pltpu.make_async_remote_copy(
            src_ref=panel.at[shard, c], dst_ref=panel.at[shard, c],
            send_sem=ring_send.at[way, step, c], recv_sem=ring_recv.at[way, step, c],
            device_id=(me, right if way == 0 else left), device_id_type=MESH,
        ), shard

    for c in range(2):
        for way in range(2):
            if hops[way] > 0:
                ring(way, 0, c).start()

    @pl.loop(1, tiles)
    def _(k):
        to_tile(req_ref, asked, ask_send, ask_recv, lax.rem(me + k, tiles), me).start()

    asked[me] = req_ref[me]

    def spread(c, shard, values):
        for h in range(shard_rows // 16):
            for t in range(values.shape[1] // sub_cols):
                cells[c, shard * (shard_rows // 16) + h, t] = values[
                    h * 16 : (h + 1) * 16, t * sub_cols : (t + 1) * sub_cols
                ]

    for c in range(2):
        spread(c, tm, model_ref[c])
    for step in range(hops[0]):
        for c in range(2):
            for way in range(2):
                if step < hops[way]:
                    copy, shard = arrived(way, step, c)
                    copy.wait_recv()
                    if step + 1 < hops[way]:
                        ring(way, step + 1, c).start()
                    spread(c, shard, panel[shard, c])

    @pl.loop(1, tiles)
    def _(k):
        peer = lax.rem(me + k, tiles)
        to_tile(asked, asked, ask_send, ask_recv, peer, peer).wait_recv()

    to_smem = pltpu.make_async_copy(asked, asked_s, smem_sem)
    to_smem.start()
    to_smem.wait()

    tall, broad = sub_rows + 16, 2 * sub_cols
    row_gap = lax.broadcasted_iota(jnp.int32, (sub_rows, tall), 1) - lax.broadcasted_iota(
        jnp.int32, (sub_rows, tall), 0
    )
    col_gap = lax.broadcasted_iota(jnp.int32, (broad, sub_cols), 0) - lax.broadcasted_iota(
        jnp.int32, (broad, sub_cols), 1
    )

    def cut(peer, target):
        for s in range(slots):
            row = jnp.maximum(asked_s[peer, 0, 2 * s], 0)
            col = jnp.maximum(asked_s[peer, 0, 2 * s + 1], 0)
            top = jnp.minimum(lax.div(row, 16), cells.shape[1] - tall // 16)
            base = jnp.minimum(lax.div(col, sub_cols), cells.shape[2] - 2)
            window = jnp.concatenate(
                [
                    jnp.concatenate([cells[c, top + i, base + j] for c in range(2) for j in range(2)], axis=1)
                    for i in range(tall // 16)
                ],
                axis=0,
            )
            pick_rows = (row_gap == row - 16 * top).astype(jnp.float32).astype(jnp.bfloat16)
            pick_cols = (col_gap == col - sub_cols * base).astype(jnp.float32).astype(jnp.bfloat16)
            window = jnp.dot(pick_rows, window, preferred_element_type=jnp.float32).astype(jnp.bfloat16)
            window = jnp.concatenate([window[:, :broad], window[:, broad:]], axis=0)
            window = jnp.dot(window, pick_cols, preferred_element_type=jnp.float32).astype(jnp.bfloat16)
            target[peer, s] = window.reshape(2, sub_rows, sub_cols)

    @pl.loop(0, (tiles - 1) // width)
    def _(i):
        peers = [lax.rem(me + 1 + i * width + w, tiles) for w in range(width)]
        for peer in peers:
            cut(peer, patch_out)
        for peer in peers:
            to_tile(patch_out, patch_in, patch_send, patch_recv, peer, me).start()

    cut(me, patch_in)
    for load in loads + lists:
        load.wait()

    def work(peer, target):
        for s in range(slots):
            b = jnp.maximum(req_s[peer, 0, 2 * slots + s], 0)
            patch = patch_in[peer, s].reshape(2 * sub_rows, sub_cols)
            cols = cols_ref[b]
            sampled = jnp.dot(patch, cols, preferred_element_type=jnp.float32)
            weights = rows_ref[b].astype(jnp.float32)
            sampled = sampled.reshape(2, sub_rows, vis_n)
            predicted = jnp.sum(weights[None] * sampled, axis=1)
            residual = vis_ref[b].astype(jnp.float32) - predicted
            res_slots[peer * slots + s] = residual
            weighted = (weights[None] * residual[:, None, :]).astype(jnp.bfloat16)
            weighted = weighted.reshape(2 * sub_rows, vis_n)
            sub = lax.dot_general(
                weighted, cols, (((1,), (1,)), ((), ())), preferred_element_type=jnp.float32
            )
            sub = sub.astype(jnp.bfloat16).reshape(2, sub_rows, sub_cols)
            for c in range(2):
                target[c, peer, s] = sub[c]

    work(me, back_ref)
    acc[...] = jnp.zeros_like(acc)

    @pl.loop(0, (tiles - 1) // width)
    def _(i):
        peers = [lax.rem(me + tiles - 1 - i * width - w, tiles) for w in range(width)]
        for peer in peers:
            to_tile(patch_out, patch_in, patch_send, patch_recv, peer, peer).wait_recv()
        for peer in peers:
            work(peer, sub_out)
        for peer in peers:
            give_back(0, peer, me).start()

    @pl.loop(1, tiles)
    def _(k):
        give_back(1, lax.rem(me + tiles - k, tiles), me).start()

    @pl.loop(0, res_ref.shape[0], unroll=4)
    def _(b):
        res_ref[b] = res_slots[pos_s[0, b]]

    chunk = acc.shape[3]
    halves = acc.shape[1]
    tile_rows = acc.shape[2]

    def sum_copy(c, h, way, step):
        length = hops[way ^ h]
        away = length - step
        shard = lax.rem(tm - away + group, group) if way == 0 else lax.rem(tm + away, group)
        rows = pl.ds(pl.multiple_of(shard * shard_rows, shard_rows), shard_rows)
        src = acc.at[c, h, rows] if step == 0 else sums.at[c, h, way, step - 1]
        copy = pltpu.make_async_remote_copy(
            src_ref=src, dst_ref=sums.at[c, h, way, step],
            send_sem=sum_send.at[c, h, way, step], recv_sem=sum_recv.at[c, h, way, step],
            device_id=(me, left if way == 0 else right), device_id_type=MESH,
        )
        return copy, rows

    chains = [(h, way) for h in range(halves) for way in range(2) if hops[way ^ h] > 0]

    def sum_step(c, step):
        for h, way in chains:
            length = hops[way ^ h]
            if step > 0 and step <= length:
                sum_copy(c, h, way, step - 1)[0].wait_recv()
            if step < length:
                copy, rows = sum_copy(c, h, way, step)
                if step > 0:
                    sums[c, h, way, step - 1] += acc[c, h, rows]
                copy.start()
        if step == max(hops):
            own = pl.ds(pl.multiple_of(tm * shard_rows, shard_rows), shard_rows)
            for h in range(halves):
                total = acc[c, h, own]
                for way in range(2):
                    if hops[way ^ h] > 0:
                        total += sums[c, h, way, hops[way ^ h] - 1]
                out_ref[c, :, h * chunk : (h + 1) * chunk] = total

    batch = min(8, tiles)
    turns = tiles // batch
    lane = lax.broadcasted_iota(jnp.int32, (1, 128), 1)
    grid_row = lax.broadcasted_iota(jnp.int32, (tile_rows, 128), 0)
    place_gap = lax.broadcasted_iota(jnp.int32, (sub_cols, broad), 1) - lax.broadcasted_iota(
        jnp.int32, (sub_cols, broad), 0
    )
    per = 128 // sub_rows
    col_tiles = spread_ref.shape[1] // sub_cols

    def add_batch(c, i):
        starts = []
        for w in range(batch):
            k = i * batch + w
            peer = lax.rem(me + k, tiles)

            @pl.when(k > 0)
            def _():
                give_back(c, peer, peer).wait_recv()

        for w in range(batch):
            peer = lax.rem(me + i * batch + w, tiles)
            for s in range(slots):
                row = asked_s[peer, 0, 2 * s]
                col = jnp.maximum(asked_s[peer, 0, 2 * s + 1], 0)
                starts.append(jnp.where(row < 0, -4 * tile_rows, row))
                base = jnp.minimum(lax.div(col, sub_cols), col_tiles - 2)
                put = (place_gap == col - sub_cols * base).astype(jnp.float32).astype(jnp.bfloat16)
                moved = jnp.dot(back_ref[c, peer, s], put, preferred_element_type=jnp.float32)
                at = (w * slots + s) * sub_rows
                where = jnp.broadcast_to(base, (sub_rows, sub_cols))
                low, high = moved[:, :sub_cols], moved[:, sub_cols:]
                for t in range(col_tiles):
                    piece = jnp.where(where == t, low, jnp.where(where == t - 1, high, 0.0))
                    spread_ref[at : at + sub_rows, t * sub_cols : (t + 1) * sub_cols] = piece.astype(jnp.bfloat16)
        hot = []
        for q in range(0, len(starts), per):
            first = jnp.broadcast_to(starts[q + per - 1], (1, 128))
            for r in range(per - 2, -1, -1):
                first = jnp.where(lane < (r + 1) * sub_rows, starts[q + r], first)
            first = first + lax.rem(lane, sub_rows)
            hot.append((grid_row == first).astype(jnp.float32).astype(jnp.bfloat16))
        hot = jnp.concatenate(hot, axis=1)
        for h in range(halves):
            for n in range(0, chunk, 256):
                at = h * chunk + n
                acc[c, h, :, n : n + 256] += jnp.dot(
                    hot, spread_ref[:, at : at + 256], preferred_element_type=jnp.float32
                )

    @pl.loop(0, 2 * turns)
    def _(j):
        add_batch(j // turns, lax.rem(j, turns))
        for step in range(max(hops)):

            @pl.when(j == turns - 1 + step * turns // max(hops))
            def _():
                sum_step(0, step)

    sum_step(1, 0)
    sum_step(0, max(hops))
    for step in range(max(hops)):
        sum_step(1, step + 1)

    for c in range(2):
        for way in range(2):
            for step in range(hops[way]):
                ring(way, step, c).wait_send()
        for h, way in chains:
            for step in range(hops[way ^ h]):
                sum_copy(c, h, way, step)[0].wait_send()

    @pl.loop(1, tiles)
    def _(k):
        peer = lax.rem(me + k, tiles)
        to_tile(req_ref, asked, ask_send, ask_recv, peer, me).wait_send()
        to_tile(patch_out, patch_in, patch_send, patch_recv, peer, me).wait_send()
        for c in range(2):
            give_back(c, peer, me).wait_send()


def smem():
    return pl.BlockSpec(memory_space=pltpu.SMEM)


def vmem():
    return pl.BlockSpec(memory_space=pltpu.VMEM)


def anywhere():
    return pl.BlockSpec(memory_space=pl.ANY)


def shards(model, kern_rows, kern_cols, visibilities, owner_tile, row_offset, col_offset):
    tiles = lax.axis_size("tile")
    group = lax.axis_size("tm")
    blocks = owner_tile.shape[0]
    slots = (blocks + tiles - 1) // tiles + 1
    sub_rows = kern_rows.shape[1]
    sub_cols = kern_cols.shape[1]
    vis_n = kern_rows.shape[2]
    shard_rows, grid_cols = model.shape[1:]
    tile_rows = group * shard_rows

    pair = (tiles, slots, 2, sub_rows, sub_cols)
    hops = max(group // 2, 1)
    dma = pltpu.SemaphoreType.DMA
    back = (2, tiles, slots, sub_rows, sub_cols)
    batch = min(8, tiles)
    return pl.pallas_call(
        functools.partial(major_kernel, tiles, group, slots),
        out_shape=[
            jax.ShapeDtypeStruct((2, shard_rows, grid_cols), jnp.float32),
            jax.ShapeDtypeStruct((blocks, 2, vis_n), jnp.float32),
        ],
        in_specs=[anywhere()] * 7,
        out_specs=[vmem(), vmem()],
        scratch_shapes=[
            pltpu.VMEM((3, 1, blocks), jnp.int32),
            pltpu.VMEM(model.shape, jnp.bfloat16),
            pltpu.VMEM((tiles, 1, 128), jnp.int32),
            pltpu.VMEM((1, 128), jnp.int32),
            pltpu.SMEM((tiles, 1, 128), jnp.int32),
            pltpu.SMEM((1, 128), jnp.int32),
            pltpu.VMEM((tiles, 1, 128), jnp.int32),
            pltpu.VMEM((group, 2, shard_rows, grid_cols), jnp.bfloat16),
            pltpu.VMEM((2, tile_rows // 16, grid_cols // sub_cols, 16, sub_cols), jnp.bfloat16),
            pltpu.SMEM((tiles, 1, 128), jnp.int32),
            pltpu.VMEM(pair, jnp.bfloat16),
            pltpu.VMEM(pair, jnp.bfloat16),
            pltpu.VMEM(back, jnp.bfloat16),
            pltpu.VMEM(back, jnp.bfloat16),
            pltpu.VMEM(kern_rows.shape, jnp.bfloat16),
            pltpu.VMEM(kern_cols.shape, jnp.bfloat16),
            pltpu.VMEM(visibilities.shape, jnp.bfloat16),
            pltpu.VMEM((tiles * slots, 2, vis_n), jnp.float32),
            pltpu.VMEM((batch * slots * sub_rows, grid_cols), jnp.bfloat16),
            pltpu.VMEM((2, 2, tile_rows, grid_cols // 2), jnp.float32),
            pltpu.VMEM((2, 2, 2, hops, shard_rows, grid_cols // 2), jnp.float32),
            dma((3,)),
            dma((6,)),
            dma,
            dma((tiles,)),
            dma((tiles,)),
            dma((2, hops, 2)),
            dma((2, hops, 2)),
            dma((tiles,)),
            dma((tiles,)),
            dma((2, tiles)),
            dma((2, tiles)),
            dma((2, 2, 2, hops)),
            dma((2, 2, 2, hops)),
        ],
        compiler_params=pltpu.CompilerParams(
            collective_id=0, has_side_effects=True, vmem_limit_bytes=VMEM_LIMIT
        ),
        name="major",
    )(
        owner_tile.reshape(1, blocks), row_offset.reshape(1, blocks), col_offset.reshape(1, blocks),
        model, kern_rows, kern_cols, visibilities,
    )


def solution(mesh):
    placed = (
        P(None, ("tile", "tm"), None),
        P(("tile", "tm"), None, None),
        P(("tile", "tm"), None, None),
        P(("tile", "tm"), None, None),
        P(("tile", "tm"), None),
        P(("tile", "tm")),
        P(("tile", "tm")),
    )
    return jax.shard_map(
        shards,
        mesh=mesh,
        in_specs=placed,
        out_specs=(P(None, ("tile", "tm"), None), P(("tile", "tm"), None, None)),
        check_vma=False,
    )
```

```python
import functools

import jax
import jax.numpy as jnp
from jax import lax
from jax.experimental import pallas as pl
from jax.experimental.pallas import tpu as pltpu
from jax.sharding import PartitionSpec as P

VMEM_LIMIT = 63 * 1024 * 1024
MESH = pl.DeviceIdType.MESH


def major_kernel(
    tiles, group, slots,
    owner_hbm, row_hbm, col_hbm, model_hbm, rows_hbm, cols_hbm, vis_hbm,
    out_ref, res_ref,
    wanted, model_ref, req_ref, pos_v, req_s, pos_s, asked, panel, cells, asked_s, patch_out, patch_in, sub_out, back_ref, rows_ref, cols_ref, vis_ref, res_slots,
    spread_ref, acc, sums,
    kern_sem, want_sem, smem_sem, ask_send, ask_recv, ring_send, ring_recv, patch_send, patch_recv, back_send, back_recv,
    sum_send, sum_recv,
):
    me = lax.axis_index("tile")
    tm = lax.axis_index("tm")
    blocks = res_ref.shape[0]
    sub_rows, sub_cols = patch_in.shape[3], patch_in.shape[4]
    shard_rows = model_ref.shape[1]
    vis_n = rows_ref.shape[2]
    right, left = lax.rem(tm + 1, group), lax.rem(tm + group - 1, group)
    width = 3 if (tiles - 1) % 3 == 0 else 1

    first = [
        pltpu.make_async_copy(src, dst, want_sem.at[i])
        for i, (src, dst) in enumerate(
            ((owner_hbm, wanted.at[0]), (row_hbm, wanted.at[1]), (col_hbm, wanted.at[2]), (model_hbm, model_ref))
        )
    ]
    for load in first:
        load.start()
    loads = [
        pltpu.make_async_copy(src, dst, kern_sem.at[i])
        for i, (src, dst) in enumerate(((rows_hbm, rows_ref), (cols_hbm, cols_ref), (vis_hbm, vis_ref)))
    ]
    for load in loads:
        load.start()

    barrier = pltpu.get_barrier_semaphore()

    @pl.loop(1, tiles)
    def _(k):
        pl.semaphore_signal(barrier, inc=1, device_id=(lax.rem(me + k, tiles), tm), device_id_type=MESH)

    near = [right, left] if group > 2 else [right]
    for other in near:
        pl.semaphore_signal(barrier, inc=1, device_id=(me, other), device_id_type=MESH)
    for load in first:
        load.wait()
    owner, row_at, col_at = wanted[0], wanted[1], wanted[2]
    ids = lax.broadcasted_iota(jnp.int32, (1, blocks), 1)
    down = lax.broadcasted_iota(jnp.int32, (blocks, blocks), 0)
    along = lax.broadcasted_iota(jnp.int32, (blocks, blocks), 1)
    owner_down = jnp.sum(jnp.where(down == along, owner, 0), axis=1, keepdims=True)
    earlier = jnp.where((owner_down == owner) & (down < along), 1, 0)
    place = owner * slots + jnp.sum(earlier, axis=0, keepdims=True)
    lanes = lax.broadcasted_iota(jnp.int32, (tiles, 128), 1)
    tile_at = lax.broadcasted_iota(jnp.int32, (tiles, blocks), 0) * slots
    request = jnp.zeros((tiles, 128), jnp.int32)
    for s in range(slots):
        hot = tile_at + s == place
        for lane_at, value in ((2 * s, row_at + 1), (2 * s + 1, col_at + 1), (2 * slots + s, ids + 1)):
            found = jnp.sum(jnp.where(hot, value, 0), axis=1, keepdims=True) - 1
            request = jnp.where(lanes == lane_at, found, request)
    req_ref[...] = request.reshape(tiles, 1, 128)
    pos_v[...] = jnp.concatenate([place, jnp.zeros((1, 128 - blocks), jnp.int32)], axis=1)
    lists = [
        pltpu.make_async_copy(src, dst, want_sem.at[4 + i])
        for i, (src, dst) in enumerate(((req_ref, req_s), (pos_v, pos_s)))
    ]
    for load in lists:
        load.start()
    pl.semaphore_wait(barrier, tiles - 1 + len(near))

    def to_tile(src, dst, send, recv, peer, mine):
        return pltpu.make_async_remote_copy(
            src_ref=src.at[peer], dst_ref=dst.at[mine], send_sem=send.at[peer], recv_sem=recv.at[mine],
            device_id=(peer, tm), device_id_type=MESH,
        )

    def give_back(c, peer, mine):
        return pltpu.make_async_remote_copy(
            src_ref=sub_out.at[c, peer], dst_ref=back_ref.at[c, mine],
            send_sem=back_send.at[c, peer], recv_sem=back_recv.at[c, mine],
            device_id=(peer, tm), device_id_type=MESH,
        )

    def ring(way, step, c):
        shard = lax.rem(tm - step + group, group) if way == 0 else lax.rem(tm + step, group)
        src = model_ref.at[c] if step == 0 else panel.at[shard, c]
        return pltpu.make_async_remote_copy(
            src_ref=src, dst_ref=panel.at[shard, c],
            send_sem=ring_send.at[way, step, c], recv_sem=ring_recv.at[way, step, c],
            device_id=(me, right if way == 0 else left), device_id_type=MESH,
        )

    hops = (group // 2, (group - 1) // 2)

    def arrived(way, step, c):
        shard = lax.rem(tm - step - 1 + group, group) if way == 0 else lax.rem(tm + step + 1, group)
        return pltpu.make_async_remote_copy(
            src_ref=panel.at[shard, c], dst_ref=panel.at[shard, c],
            send_sem=ring_send.at[way, step, c], recv_sem=ring_recv.at[way, step, c],
            device_id=(me, right if way == 0 else left), device_id_type=MESH,
        ), shard

    for c in range(2):
        for way in range(2):
            if hops[way] > 0:
                ring(way, 0, c).start()

    @pl.loop(1, tiles)
    def _(k):
        to_tile(req_ref, asked, ask_send, ask_recv, lax.rem(me + k, tiles), me).start()

    asked[me] = req_ref[me]

    def spread(c, shard, values):
        for h in range(shard_rows // 16):
            for t in range(values.shape[1] // sub_cols):
                cells[c, shard * (shard_rows // 16) + h, t] = values[
                    h * 16 : (h + 1) * 16, t * sub_cols : (t + 1) * sub_cols
                ]

    for c in range(2):
        spread(c, tm, model_ref[c])
    for step in range(hops[0]):
        for c in range(2):
            for way in range(2):
                if step < hops[way]:
                    copy, shard = arrived(way, step, c)
                    copy.wait_recv()
                    if step + 1 < hops[way]:
                        ring(way, step + 1, c).start()
                    spread(c, shard, panel[shard, c])

    @pl.loop(1, tiles)
    def _(k):
        peer = lax.rem(me + k, tiles)
        to_tile(asked, asked, ask_send, ask_recv, peer, peer).wait_recv()

    to_smem = pltpu.make_async_copy(asked, asked_s, smem_sem)
    to_smem.start()
    to_smem.wait()

    tall, broad = sub_rows + 16, 2 * sub_cols
    row_gap = lax.broadcasted_iota(jnp.int32, (sub_rows, tall), 1) - lax.broadcasted_iota(
        jnp.int32, (sub_rows, tall), 0
    )
    col_gap = lax.broadcasted_iota(jnp.int32, (broad, sub_cols), 0) - lax.broadcasted_iota(
        jnp.int32, (broad, sub_cols), 1
    )

    def cut(peer, target):
        for s in range(slots):
            row = jnp.maximum(asked_s[peer, 0, 2 * s], 0)
            col = jnp.maximum(asked_s[peer, 0, 2 * s + 1], 0)
            top = jnp.minimum(lax.div(row, 16), cells.shape[1] - tall // 16)
            base = jnp.minimum(lax.div(col, sub_cols), cells.shape[2] - 2)
            window = jnp.concatenate(
                [
                    jnp.concatenate([cells[c, top + i, base + j] for c in range(2) for j in range(2)], axis=1)
                    for i in range(tall // 16)
                ],
                axis=0,
            )
            pick_rows = (row_gap == row - 16 * top).astype(jnp.float32).astype(jnp.bfloat16)
            pick_cols = (col_gap == col - sub_cols * base).astype(jnp.float32).astype(jnp.bfloat16)
            window = jnp.dot(pick_rows, window, preferred_element_type=jnp.float32).astype(jnp.bfloat16)
            window = jnp.concatenate([window[:, :broad], window[:, broad:]], axis=0)
            window = jnp.dot(window, pick_cols, preferred_element_type=jnp.float32).astype(jnp.bfloat16)
            target[peer, s] = window.reshape(2, sub_rows, sub_cols)

    @pl.loop(0, (tiles - 1) // width)
    def _(i):
        peers = [lax.rem(me + 1 + i * width + w, tiles) for w in range(width)]
        for peer in peers:
            cut(peer, patch_out)
        for peer in peers:
            to_tile(patch_out, patch_in, patch_send, patch_recv, peer, me).start()

    cut(me, patch_in)
    for load in loads + lists:
        load.wait()

    def work(peer, target):
        for s in range(slots):
            b = jnp.maximum(req_s[peer, 0, 2 * slots + s], 0)
            patch = patch_in[peer, s].reshape(2 * sub_rows, sub_cols)
            cols = cols_ref[b]
            sampled = jnp.dot(patch, cols, preferred_element_type=jnp.float32)
            weights = rows_ref[b].astype(jnp.float32)
            sampled = sampled.reshape(2, sub_rows, vis_n)
            predicted = jnp.sum(weights[None] * sampled, axis=1)
            residual = vis_ref[b].astype(jnp.float32) - predicted
            res_slots[peer * slots + s] = residual
            weighted = (weights[None] * residual[:, None, :]).astype(jnp.bfloat16)
            weighted = weighted.reshape(2 * sub_rows, vis_n)
            sub = lax.dot_general(
                weighted, cols, (((1,), (1,)), ((), ())), preferred_element_type=jnp.float32
            )
            sub = sub.astype(jnp.bfloat16).reshape(2, sub_rows, sub_cols)
            for c in range(2):
                target[c, peer, s] = sub[c]

    work(me, back_ref)
    acc[...] = jnp.zeros_like(acc)

    @pl.loop(0, (tiles - 1) // width)
    def _(i):
        peers = [lax.rem(me + tiles - 1 - i * width - w, tiles) for w in range(width)]
        for peer in peers:
            to_tile(patch_out, patch_in, patch_send, patch_recv, peer, peer).wait_recv()
        for peer in peers:
            work(peer, sub_out)
        for peer in peers:
            give_back(0, peer, me).start()

    @pl.loop(1, tiles)
    def _(k):
        give_back(1, lax.rem(me + tiles - k, tiles), me).start()

    @pl.loop(0, res_ref.shape[0], unroll=4)
    def _(b):
        res_ref[b] = res_slots[pos_s[0, b]]

    chunk = acc.shape[3]
    halves = acc.shape[1]
    tile_rows = acc.shape[2]

    def sum_copy(c, h, way, step):
        length = hops[way ^ h]
        away = length - step
        shard = lax.rem(tm - away + group, group) if way == 0 else lax.rem(tm + away, group)
        rows = pl.ds(pl.multiple_of(shard * shard_rows, shard_rows), shard_rows)
        src = acc.at[c, h, rows] if step == 0 else sums.at[c, h, way, step - 1]
        copy = pltpu.make_async_remote_copy(
            src_ref=src, dst_ref=sums.at[c, h, way, step],
            send_sem=sum_send.at[c, h, way, step], recv_sem=sum_recv.at[c, h, way, step],
            device_id=(me, left if way == 0 else right), device_id_type=MESH,
        )
        return copy, rows

    chains = [(h, way) for h in range(halves) for way in range(2) if hops[way ^ h] > 0]

    def sum_step(c, step):
        for h, way in chains:
            length = hops[way ^ h]
            if step > 0 and step <= length:
                sum_copy(c, h, way, step - 1)[0].wait_recv()
            if step < length:
                copy, rows = sum_copy(c, h, way, step)
                if step > 0:
                    sums[c, h, way, step - 1] += acc[c, h, rows]
                copy.start()
        if step == max(hops):
            own = pl.ds(pl.multiple_of(tm * shard_rows, shard_rows), shard_rows)
            for h in range(halves):
                total = acc[c, h, own]
                for way in range(2):
                    if hops[way ^ h] > 0:
                        total += sums[c, h, way, hops[way ^ h] - 1]
                out_ref[c, :, h * chunk : (h + 1) * chunk] = total

    batch = min(4, tiles)
    turns = tiles // batch
    lane = lax.broadcasted_iota(jnp.int32, (1, 128), 1)
    grid_row = lax.broadcasted_iota(jnp.int32, (tile_rows, 128), 0)
    place_gap = lax.broadcasted_iota(jnp.int32, (sub_cols, broad), 1) - lax.broadcasted_iota(
        jnp.int32, (sub_cols, broad), 0
    )
    per = 128 // sub_rows
    col_tiles = spread_ref.shape[1] // sub_cols

    def add_batch(c, i):
        starts = []
        for w in range(batch):
            k = i * batch + w
            peer = lax.rem(me + k, tiles)

            @pl.when(k > 0)
            def _():
                give_back(c, peer, peer).wait_recv()

        for w in range(batch):
            peer = lax.rem(me + i * batch + w, tiles)
            for s in range(slots):
                row = asked_s[peer, 0, 2 * s]
                col = jnp.maximum(asked_s[peer, 0, 2 * s + 1], 0)
                starts.append(jnp.where(row < 0, -4 * tile_rows, row))
                base = jnp.minimum(lax.div(col, sub_cols), col_tiles - 2)
                put = (place_gap == col - sub_cols * base).astype(jnp.float32).astype(jnp.bfloat16)
                moved = jnp.dot(back_ref[c, peer, s], put, preferred_element_type=jnp.float32)
                at = (w * slots + s) * sub_rows
                where = jnp.broadcast_to(base, (sub_rows, sub_cols))
                low, high = moved[:, :sub_cols], moved[:, sub_cols:]
                for t in range(col_tiles):
                    piece = jnp.where(where == t, low, jnp.where(where == t - 1, high, 0.0))
                    spread_ref[at : at + sub_rows, t * sub_cols : (t + 1) * sub_cols] = piece.astype(jnp.bfloat16)
        hot = []
        for q in range(0, len(starts), per):
            first = jnp.broadcast_to(starts[q + per - 1], (1, 128))
            for r in range(per - 2, -1, -1):
                first = jnp.where(lane < (r + 1) * sub_rows, starts[q + r], first)
            first = first + lax.rem(lane, sub_rows)
            hot.append((grid_row == first).astype(jnp.float32).astype(jnp.bfloat16))
        hot = jnp.concatenate(hot, axis=1)
        for h in range(halves):
            for n in range(0, chunk, 256):
                at = h * chunk + n
                acc[c, h, :, n : n + 256] += jnp.dot(
                    hot, spread_ref[:, at : at + 256], preferred_element_type=jnp.float32
                )

    @pl.loop(0, 2 * turns)
    def _(j):
        add_batch(j // turns, lax.rem(j, turns))
        for step in range(max(hops)):

            @pl.when(j == turns - 1 + step * turns // max(hops))
            def _():
                sum_step(0, step)

    sum_step(1, 0)
    sum_step(0, max(hops))
    for step in range(max(hops)):
        sum_step(1, step + 1)

    for c in range(2):
        for way in range(2):
            for step in range(hops[way]):
                ring(way, step, c).wait_send()
        for h, way in chains:
            for step in range(hops[way ^ h]):
                sum_copy(c, h, way, step)[0].wait_send()

    @pl.loop(1, tiles)
    def _(k):
        peer = lax.rem(me + k, tiles)
        to_tile(req_ref, asked, ask_send, ask_recv, peer, me).wait_send()
        to_tile(patch_out, patch_in, patch_send, patch_recv, peer, me).wait_send()
        for c in range(2):
            give_back(c, peer, me).wait_send()


def smem():
    return pl.BlockSpec(memory_space=pltpu.SMEM)


def vmem():
    return pl.BlockSpec(memory_space=pltpu.VMEM)


def anywhere():
    return pl.BlockSpec(memory_space=pl.ANY)


def shards(model, kern_rows, kern_cols, visibilities, owner_tile, row_offset, col_offset):
    tiles = lax.axis_size("tile")
    group = lax.axis_size("tm")
    blocks = owner_tile.shape[0]
    slots = (blocks + tiles - 1) // tiles + 1
    sub_rows = kern_rows.shape[1]
    sub_cols = kern_cols.shape[1]
    vis_n = kern_rows.shape[2]
    shard_rows, grid_cols = model.shape[1:]
    tile_rows = group * shard_rows

    pair = (tiles, slots, 2, sub_rows, sub_cols)
    hops = max(group // 2, 1)
    dma = pltpu.SemaphoreType.DMA
    back = (2, tiles, slots, sub_rows, sub_cols)
    batch = min(4, tiles)
    return pl.pallas_call(
        functools.partial(major_kernel, tiles, group, slots),
        out_shape=[
            jax.ShapeDtypeStruct((2, shard_rows, grid_cols), jnp.float32),
            jax.ShapeDtypeStruct((blocks, 2, vis_n), jnp.float32),
        ],
        in_specs=[anywhere()] * 7,
        out_specs=[vmem(), vmem()],
        scratch_shapes=[
            pltpu.VMEM((3, 1, blocks), jnp.int32),
            pltpu.VMEM(model.shape, jnp.bfloat16),
            pltpu.VMEM((tiles, 1, 128), jnp.int32),
            pltpu.VMEM((1, 128), jnp.int32),
            pltpu.SMEM((tiles, 1, 128), jnp.int32),
            pltpu.SMEM((1, 128), jnp.int32),
            pltpu.VMEM((tiles, 1, 128), jnp.int32),
            pltpu.VMEM((group, 2, shard_rows, grid_cols), jnp.bfloat16),
            pltpu.VMEM((2, tile_rows // 16, grid_cols // sub_cols, 16, sub_cols), jnp.bfloat16),
            pltpu.SMEM((tiles, 1, 128), jnp.int32),
            pltpu.VMEM(pair, jnp.bfloat16),
            pltpu.VMEM(pair, jnp.bfloat16),
            pltpu.VMEM(back, jnp.bfloat16),
            pltpu.VMEM(back, jnp.bfloat16),
            pltpu.VMEM(kern_rows.shape, jnp.bfloat16),
            pltpu.VMEM(kern_cols.shape, jnp.bfloat16),
            pltpu.VMEM(visibilities.shape, jnp.bfloat16),
            pltpu.VMEM((tiles * slots, 2, vis_n), jnp.float32),
            pltpu.VMEM((batch * slots * sub_rows, grid_cols), jnp.bfloat16),
            pltpu.VMEM((2, 2, tile_rows, grid_cols // 2), jnp.float32),
            pltpu.VMEM((2, 2, 2, hops, shard_rows, grid_cols // 2), jnp.float32),
            dma((3,)),
            dma((6,)),
            dma,
            dma((tiles,)),
            dma((tiles,)),
            dma((2, hops, 2)),
            dma((2, hops, 2)),
            dma((tiles,)),
            dma((tiles,)),
            dma((2, tiles)),
            dma((2, tiles)),
            dma((2, 2, 2, hops)),
            dma((2, 2, 2, hops)),
        ],
        compiler_params=pltpu.CompilerParams(
            collective_id=0, has_side_effects=True, vmem_limit_bytes=VMEM_LIMIT
        ),
        name="major",
    )(
        owner_tile.reshape(1, blocks), row_offset.reshape(1, blocks), col_offset.reshape(1, blocks),
        model, kern_rows, kern_cols, visibilities,
    )


def solution(mesh):
    placed = (
        P(None, ("tile", "tm"), None),
        P(("tile", "tm"), None, None),
        P(("tile", "tm"), None, None),
        P(("tile", "tm"), None, None),
        P(("tile", "tm"), None),
        P(("tile", "tm")),
        P(("tile", "tm")),
    )
    return jax.shard_map(
        shards,
        mesh=mesh,
        in_specs=placed,
        out_specs=(P(None, ("tile", "tm"), None), P(("tile", "tm"), None, None)),
        check_vma=False,
    )
```
